256 devices in a mesh: section: 8 (over x, y_hi), replica: 4 (over y_lo, core), tensor: 8 (over z).
Axes of the slice: x: 4, y: 4 (y_hi: 2, y_lo: 2; y = y_hi * 2 + y_lo), z: 8, core: 2. Of those that a mesh axis runs over, the one named last changes fastest.
Arguments:
- up_qkv: bfloat16 [8, 4, 1024, 12288], P('section', 'replica', 'tensor'), may hold values from -8 to 8
- down_qk: bfloat16 [8, 4, 512, 2, 8192], P('section', 'replica', 'tensor'), may hold values from -8 to 8
- down_values: bfloat16 [8, 4, 512, 2, 4096], P('section', 'replica', 'tensor'), may hold values from -6 to 6
Outputs:
- up_out: bfloat16 [8, 4, 1024, 4096], P('section', 'replica', 'tensor')
- down_out: bfloat16 [8, 4, 512, 2, 4096], P('section', 'replica', 'tensor')
The draws below stay inside these ranges and needn't reach their ends.
All inputs are finite; a program needn't handle non-finite values.
Results may differ from the reference program's by a relative error of at most 0.011.
Values may be sent and summed in bfloat16 or wider, within the bound.
A program may use at most 64 MiB of HBM per device.

```python
import jax
import jax.numpy as jnp
from jax import lax

HEADS = 32
HD = 128
SEQ = 1024
SECTIONS = 8
REPLICAS = 4


def lifted_pairs(key, lead_shape, part_count, lifted_parts, top_lift, clip_at):
    noise_key, sign_key, pick_key, size_key = jax.random.split(key, 4)
    noise_draw = jax.random.normal(noise_key, lead_shape + (part_count, HEADS, HD), jnp.float32)
    noise_draw = jnp.clip(noise_draw, -clip_at, clip_at)
    sign_table = jnp.where(jax.random.bernoulli(sign_key, 0.5, (HEADS, HD)), 1.0, -1.0).astype(jnp.float32)
    picked = jax.random.bernoulli(pick_key, 0.125, lead_shape)
    strength = jax.random.uniform(size_key, lead_shape, jnp.float32, 0.5, 1.0) * top_lift
    lift_size = jnp.where(picked, strength, 0.0).astype(jnp.float32)
    part_mask = (jnp.arange(part_count) < lifted_parts).astype(jnp.float32)
    shifted = noise_draw + lift_size.reshape(lead_shape + (1, 1, 1)) * part_mask.reshape(part_count, 1, 1) * sign_table
    return shifted.reshape(lead_shape + (part_count * HEADS * HD,))


def draw_up_qkv(key, part):
    key = jax.random.fold_in(key, 11)
    return lifted_pairs(key, (SECTIONS, REPLICAS, SEQ), 3, 2, 0.0, 6.0).astype(jnp.bfloat16)


def draw_down_qk(key, part):
    key = jax.random.fold_in(key, 12)
    return lifted_pairs(key, (SECTIONS, REPLICAS, SEQ // 2, 2), 2, 2, 0.0, 6.0).astype(jnp.bfloat16)


def block_scale(rng, shape, pieces, low, high):
    gain, own = 1.0, jax.random.fold_in(rng, 6)
    for axis_at, shards_of in pieces:
        heights = jnp.exp(jax.random.uniform(jax.random.fold_in(own, axis_at), (shards_of,), jnp.float32, low / len(pieces), high / len(pieces)))
        gain = gain * jnp.repeat(heights, shape[axis_at] // shards_of).reshape([-1 if axis == axis_at else 1 for axis in range(len(shape))])
    return gain


def normal_values(own_key, extent, scale, bound, shards=(), kind=jnp.bfloat16):
    entries = scale * jax.random.normal(own_key, extent, jnp.float32)
    if shards:
        entries = entries * block_scale(own_key, extent, shards, -0.22, 0.18)
    return jnp.clip(entries, -bound, bound).astype(kind)


def setup_inputs(seed: int = 0) -> dict:
    key_list = jax.random.split(jax.random.key(seed), 4)
    return {
        "up_qkv": draw_up_qkv(jax.random.fold_in(key_list[3], 71), 0),
        "down_qk": draw_down_qk(jax.random.fold_in(key_list[3], 71), 0),
        "down_values": normal_values(key_list[2], (SECTIONS, REPLICAS, SEQ // 2, 2, HEADS * HD), 1.0, 6.0, ((0, 8), (1, 4), (2, 8))),
    }


def attend(queries, key_rows, values):
    length = queries.shape[0]
    block_rows = min(512, length)
    block_count = length // block_rows
    score_scale = 1.0 / (queries.shape[2] ** 0.5)
    key_pos = jnp.arange(length, dtype=jnp.int32)
    keys_f = key_rows.astype(jnp.float32)
    values_f = values.astype(jnp.float32)

    def one_block(block_index):
        first_row = (block_index * block_rows).astype(jnp.int32)
        query_block = lax.dynamic_slice_in_dim(queries, first_row, block_rows, 0).astype(jnp.float32)
        scores = jnp.einsum("qhd,khd->hqk", query_block, keys_f) * score_scale
        query_pos = first_row + jnp.arange(block_rows, dtype=jnp.int32)
        allowed = key_pos[None, None, :] <= query_pos[None, :, None]
        scores = jnp.where(allowed, scores, jnp.float32(-1e30))
        row_peak = jnp.max(scores, axis=2, keepdims=True)
        expsum = jnp.exp(scores - row_peak)
        weights = (expsum / jnp.sum(expsum, axis=2, keepdims=True)).astype(jnp.bfloat16)
        return jnp.einsum("hqk,khd->qhd", weights.astype(jnp.float32), values_f).astype(jnp.bfloat16)

    blocks = lax.map(one_block, jnp.arange(block_count, dtype=jnp.int32))
    return blocks.reshape(length, queries.shape[1], queries.shape[2])


def to_sequences(layout_array):
    sections_n, replicas_n, half_len, pair_n, last_width = layout_array.shape
    split_view = layout_array.reshape(sections_n, replicas_n // 2, 2, half_len, 2, last_width)
    return jnp.swapaxes(split_view, 2, 4).reshape(sections_n, replicas_n, 2 * half_len, last_width)


def to_layout(sequence_array):
    sections_n, replicas_n, length, last_width = sequence_array.shape
    split_view = sequence_array.reshape(sections_n, replicas_n // 2, 2, length // 2, 2, last_width)
    return jnp.swapaxes(split_view, 2, 4).reshape(sections_n, replicas_n, length // 2, 2, last_width)


def reference(up_qkv, down_qk, down_values):
    sections_n, replicas_n = up_qkv.shape[0], up_qkv.shape[1]
    upper_parts = up_qkv.reshape(sections_n * replicas_n, SEQ, 3, HEADS, HD)
    up_out = lax.map(lambda item: attend(item[:, 0], item[:, 1], item[:, 2]), upper_parts)
    up_out = up_out.reshape(sections_n, replicas_n, SEQ, HEADS * HD)
    carried = jnp.concatenate([jnp.zeros((1, replicas_n, SEQ, HEADS * HD), jnp.bfloat16), up_out[:-1]], axis=0)
    sequence_qk = to_sequences(down_qk)
    sequence_values = to_sequences(down_values)
    mixed_values = (sequence_values.astype(jnp.float32) + carried.astype(jnp.float32)).astype(jnp.bfloat16)
    lower_parts = sequence_qk.reshape(sections_n * replicas_n, SEQ, 2, HEADS, HD)
    mixed_heads = mixed_values.reshape(sections_n * replicas_n, SEQ, HEADS, HD)
    attended = lax.map(lambda pair: attend(pair[0][:, 0], pair[0][:, 1], pair[1]), (lower_parts, mixed_heads))
    attended = attended.reshape(sections_n, replicas_n, SEQ, HEADS * HD)
    down_out = to_layout(attended)
    return up_out, down_out
```

```python
import functools
import math

import jax
import jax.numpy as jnp
from jax import lax
from jax.experimental import pallas as pl
from jax.experimental.pallas import tpu as pltpu
from jax.sharding import PartitionSpec as P

HD = 128
QB = 256
LOG2E = 1.4426950408889634


def exchange_kernel(
    sizes,
    up_ref,
    dqk_ref,
    dv_ref,
    upo_ref,
    dno_ref,
    upbuf,
    dnbuf,
    carr,
    upres,
    dnres,
    up_ssem,
    up_rsem,
    dn_ssem,
    dn_rsem,
    uo_ssem,
    uo_rsem,
    do_ssem,
    do_rsem,
    ca_ssem,
    ca_rsem,
    own_sem,
):
    sections, tensors, rows, width = sizes
    half = rows // 2
    seq = tensors * rows
    cols = width // tensors
    heads = cols // HD
    s = lax.axis_index("section")
    r = lax.axis_index("replica")
    z = lax.axis_index("tensor")
    core = lax.rem(r, 2)
    pair = r - core
    distances = sorted(range(1, tensors), key=lambda d: -min(d, tensors - d))

    def at(other_core, other_z):
        return {"replica": pair + other_core, "tensor": other_z}

    def z_at(d):
        return lax.rem(z + d, tensors)

    def lanes(index, size):
        return pl.ds(pl.multiple_of(index * size, size), size)

    def remote(src, dst, ssem, rsem, device):
        return pltpu.make_async_remote_copy(
            src_ref=src,
            dst_ref=dst,
            send_sem=ssem,
            recv_sem=rsem,
            device_id=device,
            device_id_type=pl.DeviceIdType.MESH,
        )

    barrier = pltpu.get_barrier_semaphore()
    for d in range(tensors):
        for flip in range(2):
            if d or flip:
                other = core + flip - 2 * flip * core
                pl.semaphore_signal(
                    barrier, inc=1, device_id=at(other, z_at(d)), device_id_type=pl.DeviceIdType.MESH
                )
    for step in (1, sections - 1):
        pl.semaphore_signal(
            barrier,
            inc=1,
            device_id={"section": lax.rem(s + step, sections)},
            device_id_type=pl.DeviceIdType.MESH,
        )
    pl.semaphore_wait(barrier, 2 * tensors - 1 + 2)

    def up_own(part):
        return pltpu.make_async_copy(
            up_ref.at[:, pl.ds(pl.multiple_of(part * width + z * cols, cols), cols)],
            upbuf.at[part, lanes(z, rows), :],
            own_sem.at[part],
        )

    def up_send(part, d):
        return remote(
            up_ref.at[:, pl.ds(pl.multiple_of(part * width + z_at(d) * cols, cols), cols)],
            upbuf.at[part, lanes(z, rows), :],
            up_ssem.at[part, d],
            up_rsem.at[part, d],
            at(core, z_at(d)),
        )

    def dn_source(part, other_core, other_z):
        if part < 2:
            return dqk_ref.at[other_core, :, pl.ds(pl.multiple_of(part * width + other_z * cols, cols), cols)]
        return dv_ref.at[other_core, :, lanes(other_z, cols)]

    def dn_place(part):
        return dnbuf.at[part, pl.ds(pl.multiple_of(z * rows + core * half, half), half), :]

    def dn_own(part):
        return pltpu.make_async_copy(dn_source(part, core, z), dn_place(part), own_sem.at[3 + part])

    def dn_send(part, flip, d):
        other = core + flip - 2 * flip * core
        return remote(
            dn_source(part, other, z_at(d)),
            dn_place(part),
            dn_ssem.at[part, flip, d],
            dn_rsem.at[part, flip, d],
            at(other, z_at(d)),
        )

    for part in range(3):
        up_own(part).start()
        for d in distances:
            up_send(part, d).start()
    for part in range(3):
        dn_own(part).start()

    dn_targets = [(0, d) for d in distances] + [(1, d) for d in distances] + [(1, 0)]
    for part in range(3):
        for d in distances:
            up_send(part, d).wait_send()
        for flip, d in dn_targets:
            dn_send(part, flip, d).start()

    scale = LOG2E / math.sqrt(HD)

    def attend_head(buf, out, head, position):
        at_head = lanes(head, HD)
        for block in range(seq // QB):
            first = block * QB
            q = buf[0, pl.ds(first, QB), at_head]
            keys = buf[1, pl.ds(first, QB), at_head]
            dims = (((1,), (1,)), ((), ()))
            diag = lax.dot_general(q, keys, dims, preferred_element_type=jnp.float32)
            row = position(lax.broadcasted_iota(jnp.int32, (QB, QB), 0))
            col = position(lax.broadcasted_iota(jnp.int32, (QB, QB), 1))
            diag = jnp.where(col <= row, diag, -1e30)
            peak = jnp.max(diag, axis=1, keepdims=True)
            if first:
                past = lax.dot_general(
                    q, buf[1, pl.ds(0, first), at_head], dims, preferred_element_type=jnp.float32
                )
                peak = jnp.maximum(peak, jnp.max(past, axis=1, keepdims=True))
            weights = jnp.exp2((diag - peak) * scale)
            total = jnp.sum(weights, axis=1, keepdims=True)
            mixed = jnp.dot(
                weights.astype(jnp.bfloat16),
                buf[2, pl.ds(first, QB), at_head],
                preferred_element_type=jnp.float32,
            )
            if first:
                weights = jnp.exp2((past - peak) * scale)
                total += jnp.sum(weights, axis=1, keepdims=True)
                mixed += jnp.dot(
                    weights.astype(jnp.bfloat16),
                    buf[2, pl.ds(0, first), at_head],
                    preferred_element_type=jnp.float32,
                )
            out[pl.ds(first, QB), at_head] = (mixed / total).astype(jnp.bfloat16)

    def natural(index):
        return index

    def parity_order(index):
        inside = lax.rem(index, rows)
        return index - inside + 2 * lax.rem(inside, half) + inside // half

    for part in range(3):
        up_own(part).wait()
        for d in distances:
            up_send(part, d).wait_recv()

    def up_target(head):
        return pl.ds(pl.multiple_of(z * cols + head * HD, HD), HD)

    def uo_own(head):
        return pltpu.make_async_copy(
            upres.at[lanes(z, rows), lanes(head, HD)], upo_ref.at[:, up_target(head)], own_sem.at[6]
        )

    def uo_send(head, d):
        return remote(
            upres.at[lanes(z_at(d), rows), lanes(head, HD)],
            upo_ref.at[:, up_target(head)],
            uo_ssem.at[head, d],
            uo_rsem.at[head, d],
            at(core, z_at(d)),
        )

    def ca_send(head):
        return remote(
            upres.at[:, lanes(head, HD)],
            carr.at[:, lanes(head, HD)],
            ca_ssem.at[head],
            ca_rsem.at[head],
            {"section": lax.rem(s + 1, sections)},
        )

    def up_head(head, carry):
        attend_head(upbuf, upres, head, natural)

        @pl.when(s < sections - 1)
        def _():
            ca_send(head).start()

        for d in distances:
            uo_send(head, d).start()
        own = uo_own(head)
        own.start()
        own.wait()
        return carry

    lax.fori_loop(0, heads, up_head, 0)

    for part in range(3):
        dn_own(part).wait()
        for flip, d in dn_targets:
            dn_send(part, flip, d).wait_recv()

    @pl.when(s > 0)
    def _():
        for head in range(heads):
            ca_send(head).wait_recv()

    @pl.when(s == 0)
    def _():
        carr[...] = jnp.zeros_like(carr)

    row = lax.broadcasted_iota(jnp.int32, (rows, rows), 0)
    col = lax.broadcasted_iota(jnp.int32, (rows, rows), 1)
    reorder = jnp.where(col == parity_order(row), 1.0, 0.0).astype(jnp.bfloat16)

    def mix(block, carry):
        here = lanes(block, rows)
        moved = jnp.dot(reorder, carr[here, :], preferred_element_type=jnp.float32)
        dnbuf[2, here, :] = (dnbuf[2, here, :].astype(jnp.float32) + moved).astype(jnp.bfloat16)
        return carry

    lax.fori_loop(0, tensors, mix, 0)

    def do_source(other_core, other_z, head):
        return dnres.at[
            pl.ds(pl.multiple_of(other_z * rows + other_core * half, half), half), lanes(head, HD)
        ]

    def do_own(head):
        return pltpu.make_async_copy(
            do_source(core, z, head), dno_ref.at[core, :, up_target(head)], own_sem.at[7]
        )

    def do_send(head, flip, d):
        other = core + flip - 2 * flip * core
        return remote(
            do_source(other, z_at(d), head),
            dno_ref.at[core, :, up_target(head)],
            do_ssem.at[head, flip, d],
            do_rsem.at[head, flip, d],
            at(other, z_at(d)),
        )

    def do_arrival(head, flip, d):
        other = core + flip - 2 * flip * core
        return remote(
            do_source(other, z_at(d), head),
            dno_ref.at[other, :, up_target(head)],
            do_ssem.at[head, flip, d],
            do_rsem.at[head, flip, d],
            at(other, z_at(d)),
        )

    def dn_head(head, carry):
        attend_head(dnbuf, dnres, head, parity_order)
        for flip, d in dn_targets:
            do_send(head, flip, d).start()
        own = do_own(head)
        own.start()
        own.wait()
        return carry

    lax.fori_loop(0, heads, dn_head, 0)

    for part in range(3):
        for flip, d in dn_targets:
            dn_send(part, flip, d).wait_send()

    def finish(head, carry):
        for d in distances:
            uo_send(head, d).wait()
        for flip, d in dn_targets:
            do_send(head, flip, d).wait_send()
            do_arrival(head, flip, d).wait_recv()

        @pl.when(s < sections - 1)
        def _():
            ca_send(head).wait_send()

        return carry

    lax.fori_loop(0, heads, finish, 0)


def per_device(mesh_sizes, up_qkv, down_qk, down_values):
    sections, tensors = mesh_sizes
    rows = up_qkv.shape[2]
    width = up_qkv.shape[3] // 3
    half = rows // 2
    seq = tensors * rows
    cols = width // tensors
    heads = cols // HD
    up = up_qkv.reshape(rows, 3 * width)
    dqk = jnp.swapaxes(down_qk.reshape(half, 2, 2 * width), 0, 1)
    dv = jnp.swapaxes(down_values.reshape(half, 2, width), 0, 1)
    hbm = pl.BlockSpec(memory_space=pl.ANY)
    dma = pltpu.SemaphoreType.DMA
    up_out, down = pl.pallas_call(
        functools.partial(exchange_kernel, (sections, tensors, rows, width)),
        name="relay",
        out_shape=(
            jax.ShapeDtypeStruct((rows, width), jnp.bfloat16),
            jax.ShapeDtypeStruct((2, half, width), jnp.bfloat16),
        ),
        in_specs=[hbm, hbm, hbm],
        out_specs=(hbm, hbm),
        scratch_shapes=[
            pltpu.VMEM((3, seq, cols), jnp.bfloat16),
            pltpu.VMEM((3, seq, cols), jnp.bfloat16),
            pltpu.VMEM((seq, cols), jnp.bfloat16),
            pltpu.VMEM((seq, cols), jnp.bfloat16),
            pltpu.VMEM((seq, cols), jnp.bfloat16),
            dma((3, tensors)),
            dma((3, tensors)),
            dma((3, 2, tensors)),
            dma((3, 2, tensors)),
            dma((heads, tensors)),
            dma((heads, tensors)),
            dma((heads, 2, tensors)),
            dma((heads, 2, tensors)),
            dma((heads,)),
            dma((heads,)),
            dma((8,)),
        ],
        compiler_params=pltpu.CompilerParams(
            collective_id=0, has_side_effects=True, vmem_limit_bytes=48 * 1024 * 1024
        ),
    )(up, dqk, dv)
    down_out = jnp.swapaxes(down, 0, 1)
    return (
        up_out.reshape(1, 1, rows, width),
        down_out.reshape(1, 1, half, 2, width),
    )


def solution(mesh):
    placed = (
        P("section", "replica", "tensor", None),
        P("section", "replica", "tensor", None, None),
        P("section", "replica", "tensor", None, None),
    )
    sizes = (mesh.shape["section"], mesh.shape["tensor"])
    return jax.shard_map(
        functools.partial(per_device, sizes),
        mesh=mesh,
        in_specs=placed,
        out_specs=(placed[0], placed[1]),
        check_vma=False,
    )
```

```python
import functools
import math

import jax
import jax.numpy as jnp
from jax import lax
from jax.experimental import pallas as pl
from jax.experimental.pallas import tpu as pltpu
from jax.sharding import PartitionSpec as P

HD = 128
ROWS = 128
NOTE = 16
RING = 8
LOG2E = 1.4426950408889634
MESH = pl.DeviceIdType.MESH

GROUPS = (
    (
        {0: (3, 1), 1: (4, 0), 2: (0, 2), 3: (0, 1), 5: (1, 0), 6: (0, 1)},
        {2: 1, 3: 5, 4: 5, 5: 4, 6: 4, 7: 4},
    ),
    (
        {0: (2, 1), 1: (3, 0), 2: (4, 0), 3: (0, 2), 4: (0, 1), 6: (1, 0)},
        {2: 1, 3: 0, 4: 6, 5: 6, 6: 5, 7: 5},
    ),
    (
        {0: (0, 3), 1: (0, 2), 2: (0, 1), 3: (1, 0), 4: (2, 0), 5: (0, 2), 6: (0, 1)},
        {4: 3, 5: 3, 6: 3, 7: 2},
    ),
    (
        {0: (0, 2), 1: (0, 1), 2: (1, 0), 3: (2, 0), 4: (3, 0), 5: (0, 2), 6: (0, 1)},
        {3: 2, 4: 2, 5: 2, 6: 1, 7: 1},
    ),
)


class Plan:
    def __init__(self, reach, visits, load):
        arcs = {}
        for j in range(RING):
            down, up = reach.get(j, (0, 0))
            arcs[j] = {(j + h) % RING for h in range(1, up + 1)} | {(j - h) % RING for h in range(1, down + 1)}
        needed = {j: set() for j in range(RING)}
        home = {i: [i] for i in range(RING)}
        away = {i: [] for i in range(RING)}
        loose = []
        for i in range(RING):
            load[i] += 1
            for j in range(i):
                spot = visits.get(i)
                here = i in arcs[j]
                there = spot is not None and (spot in arcs[j] or spot == j)
                assert here or there, (i, j)
                if here and there:
                    loose.append((i, j))
                elif here:
                    home[i].append(j)
                    needed[j].add(i)
                    load[i] += 1
                else:
                    away[i].append(j)
                    load[spot] += 1
                    if spot != j:
                        needed[j].add(spot)
        for i, j in loose:
            spot = visits[i]
            extra_home = 0 if i in needed[j] else 8
            extra_away = 0 if spot == j or spot in needed[j] else 8
            if load[i] + extra_home <= load[spot] + extra_away:
                home[i].append(j)
                needed[j].add(i)
                load[i] += 1
            else:
                away[i].append(j)
                load[spot] += 1
                if spot != j:
                    needed[j].add(spot)
        self.home = {i: sorted(home[i]) for i in home}
        self.away = {i: sorted(away[i]) for i in away}
        self.visits = {i: n for i, n in visits.items() if away[i]}
        self.slots = {n: [j for j in range(RING) if n in needed[j]] for n in range(RING)}
        self.guests = {n: [i for i in range(RING) if self.visits.get(i) == n] for n in range(RING)}
        self.edges = {n: [] for n in range(RING)}
        for j in range(RING):
            down, up = reach.get(j, (0, 0))
            for way, far in ((1, up), (-1, down)):
                last, depth = j, 0
                for h in range(1, far + 1):
                    n = (j + way * h) % RING
                    if n in needed[j]:
                        depth += 1
                        self.edges[last].append((j, n, depth))
                        last = n


def make_plans():
    load = [0] * RING
    return [Plan(reach, visits, load) for reach, visits in GROUPS], load


PLANS, LOAD = make_plans()
SLOTS = max(len(p.slots[n]) for p in PLANS for n in range(RING))
GUESTS = max(len(p.guests[n]) for p in PLANS for n in range(RING))
EDGES = max(len(p.edges[n]) for p in PLANS for n in range(RING))
DEPTH = max(e[2] for p in PLANS for n in range(RING) for e in p.edges[n])
MERGE_LAG = 2
MIX_LAG = 4
AHEAD = 1


def relay_kernel(
    sections,
    rounds,
    up_ref,
    dqk_ref,
    dv_ref,
    upo_ref,
    dno_ref,
    own,
    kv,
    guest,
    note,
    reply,
    out,
    carr,
    kv_ssem,
    kv_rsem,
    q_ssem,
    q_rsem,
    o_ssem,
    o_rsem,
    ca_ssem,
    ca_rsem,
    swap_ssem,
    swap_rsem,
    back_ssem,
    back_rsem,
    own_sem,
    put_sem,
):
    half = ROWS // 2
    groups = len(GROUPS)
    width = groups * rounds * HD
    wide = groups * HD
    scale = LOG2E / math.sqrt(HD)
    s = lax.axis_index("section")
    r = lax.axis_index("replica")
    z = lax.axis_index("tensor")
    core = lax.rem(r, 2)
    twin = r + 1 - 2 * core

    def remote(src, dst, ssem, rsem, device):
        return pltpu.make_async_remote_copy(
            src_ref=src, dst_ref=dst, send_sem=ssem, recv_sem=rsem, device_id=device, device_id_type=MESH
        )

    def stage(part):
        return pltpu.make_async_copy(up_ref.at[:, pl.ds(part * width, width)], own.at[0, part], own_sem.at[part])

    for part in (1, 2, 0):
        stage(part).start()

    barrier = pltpu.get_barrier_semaphore()
    for d in range(1, RING):
        pl.semaphore_signal(barrier, inc=1, device_id={"tensor": lax.rem(z + d, RING)}, device_id_type=MESH)
    pl.semaphore_signal(barrier, inc=1, device_id={"replica": twin}, device_id_type=MESH)
    for step in (1, sections - 1):
        pl.semaphore_signal(
            barrier, inc=1, device_id={"section": lax.rem(s + step, sections)}, device_id_type=MESH
        )
    pl.semaphore_wait(barrier, RING - 1 + 1 + 2)

    my_rows = pl.ds(pl.multiple_of(core * half, half), half)

    def down_source(part, seq):
        if part < 2:
            return dqk_ref.at[seq, :, pl.ds(part * width, width)]
        return dv_ref.at[seq]

    def keep(part):
        return pltpu.make_async_copy(down_source(part, core), own.at[1, part, my_rows, :], own_sem.at[3 + part])

    def swap(part):
        return remote(
            down_source(part, 1 - core),
            own.at[1, part, my_rows, :],
            swap_ssem.at[part],
            swap_rsem.at[part],
            {"replica": twin},
        )

    for part in (1, 0, 2):
        keep(part).start()
        swap(part).start()
    for part in range(3):
        stage(part).wait()

    def lanes(group, t):
        return pl.ds(pl.multiple_of((t * groups + group) * HD, HD), HD)

    def round_lanes(t):
        return pl.ds(pl.multiple_of(t * wide, wide), wide)

    def parity_order(index):
        return 2 * lax.rem(index, half) + index // half

    key_row = lax.broadcasted_iota(jnp.int32, (ROWS, ROWS), 0)
    query_col = lax.broadcasted_iota(jnp.int32, (ROWS, ROWS), 1)

    def partial(queries, blocks, allowed):
        scores = []
        for keys, _, diagonal in blocks:
            score = lax.dot_general(
                keys, queries, (((1,), (1,)), ((), ())), preferred_element_type=jnp.float32
            )
            scores.append(jnp.where(allowed, score, -1e30) if diagonal else score)
        peak = functools.reduce(jnp.maximum, scores)
        peak = jnp.max(peak, axis=0, keepdims=True)
        weights = [jnp.exp2((score - peak) * scale) for score in scores]
        total = jnp.sum(functools.reduce(jnp.add, weights), axis=0, keepdims=True)
        mixed = None
        for weight, (_, values, _) in zip(weights, blocks):
            term = lax.dot_general(
                values,
                weight.astype(jnp.bfloat16),
                (((0,), (0,)), ((), ())),
                preferred_element_type=jnp.float32,
            )
            mixed = term if mixed is None else mixed + term
        return mixed / total, peak * scale + jnp.log2(total)

    def program(me):
        def kv_source(layer, group, j, kind, t):
            if j == me:
                return own.at[layer, 1 + kind, :, lanes(group, t)]
            return kv.at[layer, group, PLANS[group].slots[me].index(j), kind, t]

        def kv_copy(layer, group, edge, kind, t):
            j, n, _ = PLANS[group].edges[me][edge]
            slot = PLANS[group].slots[n].index(j)
            return remote(
                kv_source(layer, group, j, kind, t),
                kv.at[layer, group, slot, kind, t],
                kv_ssem.at[layer, group, edge, kind],
                kv_rsem.at[layer, group, slot, kind, t],
                {"tensor": n},
            )

        def kv_arrival(layer, group, slot, kind, t):
            place = kv.at[layer, group, slot, kind, t]
            return remote(
                place,
                place,
                kv_ssem.at[layer, group, 0, kind],
                kv_rsem.at[layer, group, slot, kind, t],
                {"tensor": (me + 1) % RING},
            )

        def q_copy(layer, group, t):
            n = PLANS[group].visits[me]
            slot = PLANS[group].guests[n].index(me)
            return remote(
                own.at[layer, 0, :, lanes(group, t)],
                guest.at[layer, group, slot, t],
                q_ssem.at[layer, group],
                q_rsem.at[layer, group, slot, t],
                {"tensor": n},
            )

        def q_arrival(layer, group, slot, t):
            place = guest.at[layer, group, slot, t]
            return remote(
                place,
                place,
                q_ssem.at[layer, group],
                q_rsem.at[layer, group, slot, t],
                {"tensor": (me + 1) % RING},
            )

        def o_copy(layer, group, slot, t):
            i = PLANS[group].guests[me][slot]
            return remote(
                note.at[layer, group, slot, t],
                reply.at[layer, group, t],
                o_ssem.at[layer, group, slot],
                o_rsem.at[layer, group, t],
                {"tensor": i},
            )

        def o_arrival(layer, group, t):
            place = reply.at[layer, group, t]
            return remote(
                place,
                place,
                o_ssem.at[layer, group, 0],
                o_rsem.at[layer, group, t],
                {"tensor": (me + 1) % RING},
            )

        def send_kv(layer, kind, t):
            for group, plan in enumerate(PLANS):
                for edge, (j, _, _) in enumerate(plan.edges[me]):
                    if j == me:
                        kv_copy(layer, group, edge, kind, t).start()

        def send_q(layer, t):
            for group, plan in enumerate(PLANS):
                if me in plan.visits:
                    q_copy(layer, group, t).start()

        def waited(group, j):
            return any(e[0] == j for e in PLANS[group].edges[me])

        def forward(layer, t, depth):
            for group, plan in enumerate(PLANS):
                done = set()
                for edge, (j, _, deep) in enumerate(plan.edges[me]):
                    if j != me and deep == depth:
                        for kind in range(2):
                            if j not in done:
                                kv_arrival(layer, group, plan.slots[me].index(j), kind, t).wait_recv()
                            kv_copy(layer, group, edge, kind, t).start()
                        done.add(j)

        def block(layer, group, j, t):
            if j == me:
                at_head = lanes(group, t)
                return own[layer, 1, :, at_head], own[layer, 2, :, at_head], False
            slot = PLANS[group].slots[me].index(j)
            return kv[layer, group, slot, 0, t], kv[layer, group, slot, 1, t], False

        def serve(layer, t):
            for group, plan in enumerate(PLANS):
                for slot, j in enumerate(plan.slots[me]):
                    if not waited(group, j):
                        for kind in range(2):
                            kv_arrival(layer, group, slot, kind, t).wait_recv()
                for slot, i in enumerate(plan.guests[me]):
                    q_arrival(layer, group, slot, t).wait_recv()
                    blocks = [block(layer, group, j, t) for j in plan.away[i]]
                    mixed, level = partial(guest[layer, group, slot, t], blocks, None)
                    note[layer, group, slot, t, pl.ds(0, HD), :] = mixed.astype(jnp.bfloat16)
                    first = level.astype(jnp.bfloat16).astype(jnp.float32)
                    rest = level - first
                    second = rest.astype(jnp.bfloat16).astype(jnp.float32)
                    third = rest - second
                    line = lax.broadcasted_iota(jnp.int32, (NOTE, ROWS), 0)
                    tail = jnp.where(
                        line == 0, first, jnp.where(line == 1, second, jnp.where(line == 2, third, 0.0))
                    )
                    note[layer, group, slot, t, pl.ds(HD, NOTE), :] = tail.astype(jnp.bfloat16)
                    o_copy(layer, group, slot, t).start()

        def merge(layer, t):
            place = jnp.where(layer == 1, parity_order(key_row), key_row)
            against = jnp.where(layer == 1, parity_order(query_col), query_col)
            allowed = place <= against
            for group, plan in enumerate(PLANS):
                at_head = lanes(group, t)
                blocks = [block(layer, group, j, t) for j in plan.home[me] if j != me]
                blocks.append((own[layer, 1, :, at_head], own[layer, 2, :, at_head], True))
                mixed, level = partial(own[layer, 0, :, at_head], blocks, allowed)
                if me in plan.visits:
                    o_arrival(layer, group, t).wait_recv()
                    other = reply[layer, group, t, pl.ds(0, HD), :].astype(jnp.float32)
                    tail = reply[layer, group, t, pl.ds(HD, NOTE), :].astype(jnp.float32)
                    other_level = tail[0:1] + tail[1:2] + tail[2:3]
                    top = jnp.maximum(level, other_level)
                    mine = jnp.exp2(level - top)
                    theirs = jnp.exp2(other_level - top)
                    mixed = (mixed * mine + other * theirs) / (mine + theirs)
                out[layer, :, at_head] = mixed.T.astype(jnp.bfloat16)

        def put_up(t):
            return pltpu.make_async_copy(
                out.at[0, :, round_lanes(t)], upo_ref.at[:, round_lanes(t)], put_sem.at[0]
            )

        def put_down(t):
            return pltpu.make_async_copy(
                out.at[1, my_rows, round_lanes(t)], dno_ref.at[core, :, round_lanes(t)], put_sem.at[1]
            )

        def carry_on(t):
            return remote(
                out.at[0, :, round_lanes(t)],
                carr.at[:, round_lanes(t)],
                ca_ssem.at[t],
                ca_rsem.at[t],
                {"section": lax.rem(s + 1, sections)},
            )

        other_rows = pl.ds(pl.multiple_of((1 - core) * half, half), half)

        def give_back(t):
            return remote(
                out.at[1, other_rows, round_lanes(t)],
                dno_ref.at[core, :, round_lanes(t)],
                back_ssem.at[t],
                back_rsem.at[t],
                {"replica": twin},
            )

        def given_back(t):
            return remote(
                out.at[1, other_rows, round_lanes(t)],
                dno_ref.at[1 - core, :, round_lanes(t)],
                back_ssem.at[t],
                back_rsem.at[t],
                {"replica": twin},
            )

        def mix(t):
            here = round_lanes(t)

            @pl.when(s > 0)
            def _():
                carry_on(t).wait_recv()
                reorder = jnp.where(query_col == parity_order(key_row), 1.0, 0.0).astype(jnp.bfloat16)
                moved = jnp.dot(reorder, carr[:, here], preferred_element_type=jnp.float32)
                own[1, 2, :, here] = (own[1, 2, :, here].astype(jnp.float32) + moved).astype(jnp.bfloat16)

        def early(t, c):
            for kind in range(2):
                send_kv(0, kind, t)
            send_q(0, t)
            return c

        lax.fori_loop(0, AHEAD, early, 0)
        for part in range(3):
            keep(part).wait()
            swap(part).wait_recv()

        total = 2 * rounds

        def body(step, c):
            g = step - (DEPTH - 1)

            def ranged(index, low, high, act):
                @pl.when(jnp.logical_and(index >= low, index < high))
                def _():
                    act(index)

            def mix_and_send(index):
                mix(index)
                send_kv(1, 1, index)

            ahead = g + DEPTH - 1 + AHEAD
            ranged(ahead, AHEAD, rounds, lambda i: early(i, 0))

            def keys_and_queries(index):
                send_kv(1, 0, index)
                send_q(1, index)

            ranged(ahead - rounds, 0, rounds, keys_and_queries)
            ranged(g - MIX_LAG, 0, rounds, mix_and_send)
            for depth in range(2, DEPTH + 1):
                ranged(
                    g + DEPTH + 1 - depth,
                    0,
                    total,
                    lambda i, depth=depth: forward(i // rounds, lax.rem(i, rounds), depth),
                )

            def finish(index):
                layer = index // rounds
                t = lax.rem(index, rounds)
                merge(layer, t)

                @pl.when(layer == 0)
                def _():
                    put_up(t).start()

                    @pl.when(s < sections - 1)
                    def _():
                        carry_on(t).start()

                    put_up(t).wait()

                @pl.when(layer == 1)
                def _():
                    give_back(t).start()
                    put_down(t).start()
                    put_down(t).wait()

            ranged(g - MERGE_LAG, 0, total, finish)
            ranged(g, 0, total, lambda i: serve(i // rounds, lax.rem(i, rounds)))
            return c

        lax.fori_loop(0, total + DEPTH - 1 + MERGE_LAG, body, 0)

        for layer in range(2):
            for group, plan in enumerate(PLANS):
                for edge in range(len(plan.edges[me])):
                    for kind in range(2):
                        n = plan.edges[me][edge][1]
                        sent = kv.at[layer, group, 0, kind]
                        remote(
                            sent,
                            sent,
                            kv_ssem.at[layer, group, edge, kind],
                            kv_rsem.at[layer, group, 0, kind, 0],
                            {"tensor": n},
                        ).wait_send()
                if me in plan.visits:
                    sent = guest.at[layer, group, 0]
                    remote(
                        sent,
                        sent,
                        q_ssem.at[layer, group],
                        q_rsem.at[layer, group, 0, 0],
                        {"tensor": plan.visits[me]},
                    ).wait_send()
                for slot, i in enumerate(plan.guests[me]):
                    sent = note.at[layer, group, slot]
                    remote(
                        sent,
                        sent,
                        o_ssem.at[layer, group, slot],
                        o_rsem.at[layer, group, 0],
                        {"tensor": i},
                    ).wait_send()

        def settle(t, c):
            give_back(t).wait_send()
            given_back(t).wait_recv()

            @pl.when(s < sections - 1)
            def _():
                carry_on(t).wait_send()

            return c

        lax.fori_loop(0, rounds, settle, 0)
        for part in range(3):
            swap(part).wait_send()

    for me in range(RING):
        pl.when(z == me)(functools.partial(program, me))


def per_device(sections, up_qkv, down_qk, down_values):
    rows = up_qkv.shape[2]
    width = up_qkv.shape[3] // 3
    half = rows // 2
    groups = len(GROUPS)
    rounds = width // HD // groups
    up = up_qkv.reshape(rows, 3 * width)
    dqk = jnp.swapaxes(down_qk.reshape(half, 2, 2 * width), 0, 1)
    dv = jnp.swapaxes(down_values.reshape(half, 2, width), 0, 1)
    hbm = pl.BlockSpec(memory_space=pl.ANY)
    dma = pltpu.SemaphoreType.DMA

    def vmem(*shape):
        return pltpu.VMEM(shape, jnp.bfloat16)

    up_out, down = pl.pallas_call(
        functools.partial(relay_kernel, sections, rounds),
        name="relay",
        out_shape=(
            jax.ShapeDtypeStruct((rows, width), jnp.bfloat16),
            jax.ShapeDtypeStruct((2, half, width), jnp.bfloat16),
        ),
        in_specs=[hbm, hbm, hbm],
        out_specs=(hbm, hbm),
        scratch_shapes=[
            vmem(2, 3, rows, width),
            vmem(2, groups, SLOTS, 2, rounds, rows, HD),
            vmem(2, groups, GUESTS, rounds, rows, HD),
            vmem(2, groups, GUESTS, rounds, HD + NOTE, rows),
            vmem(2, groups, rounds, HD + NOTE, rows),
            vmem(2, rows, width),
            vmem(rows, width),
            dma((2, groups, EDGES, 2)),
            dma((2, groups, SLOTS, 2, rounds)),
            dma((2, groups)),
            dma((2, groups, GUESTS, rounds)),
            dma((2, groups, GUESTS)),
            dma((2, groups, rounds)),
            dma((rounds,)),
            dma((rounds,)),
            dma((3,)),
            dma((3,)),
            dma((rounds,)),
            dma((rounds,)),
            dma((6,)),
            dma((2,)),
        ],
        compiler_params=pltpu.CompilerParams(
            collective_id=0, has_side_effects=True, vmem_limit_bytes=60 * 1024 * 1024
        ),
    )(up, dqk, dv)
    down_out = jnp.swapaxes(down, 0, 1)
    return (
        up_out.reshape(1, 1, rows, width),
        down_out.reshape(1, 1, half, 2, width),
    )


def solution(mesh):
    placed = (
        P("section", "replica", "tensor", None),
        P("section", "replica", "tensor", None, None),
        P("section", "replica", "tensor", None, None),
    )
    return jax.shard_map(
        functools.partial(per_device, mesh.shape["section"]),
        mesh=mesh,
        in_specs=placed,
        out_specs=(placed[0], placed[1]),
        check_vma=False,
    )
```

```python
import functools
import math

import jax
import jax.numpy as jnp
from jax import lax
from jax.experimental import pallas as pl
from jax.experimental.pallas import tpu as pltpu
from jax.sharding import PartitionSpec as P

HD = 128
ROWS = 128
NOTE = 16
RING = 8
LOG2E = 1.4426950408889634
MESH = pl.DeviceIdType.MESH

GROUPS = (
    (
        ({0: (3, 1), 1: (4, 0), 2: (0, 2), 3: (0, 1), 5: (1, 0), 6: (0, 1)}, {2: (1,), 3: (5,), 4: (5,), 5: (4,), 6: (4,), 7: (4,)}),
    ),
    (
        ({0: (3, 1), 1: (4, 0), 2: (0, 2), 3: (0, 1), 5: (1, 0), 6: (0, 1)}, {2: (1,), 3: (5,), 4: (5,), 5: (4,), 6: (4,), 7: (4,)}),
        ({0: (0, 2), 1: (1, 1), 2: (2, 0), 3: (3, 0), 4: (0, 2), 5: (0, 1)}, {3: (2,), 4: (2,), 5: (0,), 6: (0,), 7: (6, 0)}),
    ),
    (
        ({0: (0, 3), 1: (0, 2), 2: (0, 1), 3: (1, 0), 4: (2, 0), 5: (0, 2), 6: (0, 1)}, {4: (3,), 5: (3,), 6: (3,), 7: (2,)}),
        ({0: (0, 2), 1: (0, 1), 2: (1, 0), 3: (2, 0), 4: (0, 2), 5: (0, 1)}, {3: (2,), 4: (2,), 5: (2,), 6: (1,), 7: (6, 1)}),
    ),
    (
        ({0: (0, 2), 1: (0, 1), 2: (1, 0), 3: (2, 0), 4: (3, 0), 5: (0, 1)}, {3: (2,), 4: (2,), 5: (2,), 6: (1,), 7: (6, 1)}),
        ({0: (0, 1), 1: (1, 0), 2: (2, 0), 3: (3, 0), 4: (0, 1), 6: (1, 0)}, {2: (1,), 3: (1,), 4: (1,), 5: (0,), 6: (5, 0), 7: (5, 0)}),
    ),
)


class Plan:
    def __init__(self, reach, visits, share, load):
        arcs = {}
        for j in range(RING):
            down, up = reach.get(j, (0, 0))
            arcs[j] = {(j + h) % RING for h in range(1, up + 1)} | {(j - h) % RING for h in range(1, down + 1)}
        needed = {j: set() for j in range(RING)}
        met = {i: {} for i in range(RING)}
        loose = []
        for i in range(RING):
            load[i] += share
            for j in range(i):
                spots = [n for n in (i, *visits.get(i, ())) if n in arcs[j] or n == j]
                assert spots, (i, j)
                loose.append((len(spots), i, j, spots))
        for _, i, j, spots in sorted(loose):
            best = min(spots, key=lambda n: load[n] + (0 if n == j or n in needed[j] else 8))
            met[i].setdefault(best, []).append(j)
            load[best] += share
            if best != j:
                needed[j].add(best)
        self.home = {i: sorted(met[i].get(i, [])) for i in range(RING)}
        self.visits = {i: [n for n in visits.get(i, ()) if n in met[i]] for i in range(RING)}
        self.away = {(i, n): sorted(met[i][n]) for i in range(RING) for n in self.visits[i]}
        self.slots = {n: [j for j in range(RING) if n in needed[j]] for n in range(RING)}
        self.guests = {n: [i for i in range(RING) if n in self.visits[i]] for n in range(RING)}
        self.edges = {n: [] for n in range(RING)}
        for j in range(RING):
            down, up = reach.get(j, (0, 0))
            for way, far in ((1, up), (-1, down)):
                last, depth = j, 0
                for h in range(1, far + 1):
                    n = (j + way * h) % RING
                    if n in needed[j]:
                        depth += 1
                        self.edges[last].append((j, n, depth))
                        last = n


def make_plans():
    load = [0] * RING
    return [[Plan(*table, 2 // len(tables), load) for table in tables] for tables in GROUPS], load


PLANS, LOAD = make_plans()
ALL = [plan for plans in PLANS for plan in plans]
SLOTS = max(len(p.slots[n]) for p in ALL for n in range(RING))
GUESTS = max(len(p.guests[n]) for p in ALL for n in range(RING))
EDGES = max(len(p.edges[n]) for p in ALL for n in range(RING))
VISITS = max(len(p.visits[n]) for p in ALL for n in range(RING))
DEPTH = max(e[2] for p in ALL for n in range(RING) for e in p.edges[n])
MERGE_LAG = 2
MIX_LAG = 4
AHEAD = 1


def relay_kernel(
    sections,
    rounds,
    up_ref,
    dqk_ref,
    dv_ref,
    upo_ref,
    dno_ref,
    own,
    kv,
    guest,
    note,
    reply,
    out,
    carr,
    kv_ssem,
    kv_rsem,
    q_ssem,
    q_rsem,
    o_ssem,
    o_rsem,
    ca_ssem,
    ca_rsem,
    swap_ssem,
    swap_rsem,
    back_ssem,
    back_rsem,
    own_sem,
    put_sem,
):
    half = ROWS // 2
    groups = len(GROUPS)
    width = groups * rounds * HD
    wide = groups * HD
    scale = LOG2E / math.sqrt(HD)
    s = lax.axis_index("section")
    r = lax.axis_index("replica")
    z = lax.axis_index("tensor")
    core = lax.rem(r, 2)
    twin = r + 1 - 2 * core

    def remote(src, dst, ssem, rsem, device):
        return pltpu.make_async_remote_copy(
            src_ref=src, dst_ref=dst, send_sem=ssem, recv_sem=rsem, device_id=device, device_id_type=MESH
        )

    def stage(part):
        return pltpu.make_async_copy(up_ref.at[:, pl.ds(part * width, width)], own.at[0, part], own_sem.at[part])

    for part in (1, 2, 0):
        stage(part).start()

    barrier = pltpu.get_barrier_semaphore()
    for d in range(1, RING):
        pl.semaphore_signal(barrier, inc=1, device_id={"tensor": lax.rem(z + d, RING)}, device_id_type=MESH)
    pl.semaphore_signal(barrier, inc=1, device_id={"replica": twin}, device_id_type=MESH)
    for step in (1, sections - 1):
        pl.semaphore_signal(
            barrier, inc=1, device_id={"section": lax.rem(s + step, sections)}, device_id_type=MESH
        )
    pl.semaphore_wait(barrier, RING - 1 + 1 + 2)

    my_rows = pl.ds(pl.multiple_of(core * half, half), half)

    def down_source(part, seq):
        if part < 2:
            return dqk_ref.at[seq, :, pl.ds(part * width, width)]
        return dv_ref.at[seq]

    def keep(part):
        return pltpu.make_async_copy(down_source(part, core), own.at[1, part, my_rows, :], own_sem.at[3 + part])

    def swap(part):
        return remote(
            down_source(part, 1 - core),
            own.at[1, part, my_rows, :],
            swap_ssem.at[part],
            swap_rsem.at[part],
            {"replica": twin},
        )

    for part in (1, 0, 2):
        keep(part).start()
        swap(part).start()
    for part in range(3):
        stage(part).wait()

    def lanes(group, t):
        return pl.ds(pl.multiple_of((t * groups + group) * HD, HD), HD)

    def round_lanes(t):
        return pl.ds(pl.multiple_of(t * wide, wide), wide)

    def parity_order(index):
        return 2 * lax.rem(index, half) + index // half

    key_row = lax.broadcasted_iota(jnp.int32, (ROWS, ROWS), 0)
    query_col = lax.broadcasted_iota(jnp.int32, (ROWS, ROWS), 1)

    def partial(queries, blocks, allowed):
        scores = []
        for keys, _, diagonal in blocks:
            score = lax.dot_general(
                keys, queries, (((1,), (1,)), ((), ())), preferred_element_type=jnp.float32
            )
            scores.append(jnp.where(allowed, score, -1e30) if diagonal else score)
        peak = functools.reduce(jnp.maximum, scores)
        peak = jnp.max(peak, axis=0, keepdims=True)
        weights = [jnp.exp2((score - peak) * scale) for score in scores]
        total = jnp.sum(functools.reduce(jnp.add, weights), axis=0, keepdims=True)
        mixed = None
        for weight, (_, values, _) in zip(weights, blocks):
            term = lax.dot_general(
                values,
                weight.astype(jnp.bfloat16),
                (((0,), (0,)), ((), ())),
                preferred_element_type=jnp.float32,
            )
            mixed = term if mixed is None else mixed + term
        return mixed / total, peak * scale + jnp.log2(total)

    def program(me):
        def each(t, act):
            for group, plans in enumerate(PLANS):
                for turn, plan in enumerate(plans):
                    todo = functools.partial(act, group, turn, plan)
                    if len(plans) == 1:
                        todo()
                    else:
                        pl.when(lax.rem(t, 2) == turn)(todo)

        def kv_copy(layer, group, turn, plan, edge, kind, t):
            j, n, _ = plan.edges[me][edge]
            slot = plan.slots[n].index(j)
            if j == me:
                source = own.at[layer, 1 + kind, :, lanes(group, t)]
            else:
                source = kv.at[layer, group, plan.slots[me].index(j), kind, t]
            return remote(
                source,
                kv.at[layer, group, slot, kind, t],
                kv_ssem.at[layer, group, turn, edge, kind],
                kv_rsem.at[layer, group, slot, kind, t],
                {"tensor": n},
            )

        def arrival(place, sem):
            return remote(place, place, put_sem.at[2], sem, {"tensor": (me + 1) % RING})

        def kv_arrival(layer, group, slot, kind, t):
            return arrival(kv.at[layer, group, slot, kind, t], kv_rsem.at[layer, group, slot, kind, t])

        def q_copy(layer, group, turn, plan, visit, t):
            n = plan.visits[me][visit]
            slot = plan.guests[n].index(me)
            return remote(
                own.at[layer, 0, :, lanes(group, t)],
                guest.at[layer, group, slot, t],
                q_ssem.at[layer, group, turn, visit],
                q_rsem.at[layer, group, slot, t],
                {"tensor": n},
            )

        def q_arrival(layer, group, slot, t):
            return arrival(guest.at[layer, group, slot, t], q_rsem.at[layer, group, slot, t])

        def o_copy(layer, group, turn, plan, slot, t):
            i = plan.guests[me][slot]
            visit = plan.visits[i].index(me)
            return remote(
                note.at[layer, group, slot, t],
                reply.at[layer, group, visit, t],
                o_ssem.at[layer, group, turn, slot],
                o_rsem.at[layer, group, visit, t],
                {"tensor": i},
            )

        def o_arrival(layer, group, visit, t):
            return arrival(reply.at[layer, group, visit, t], o_rsem.at[layer, group, visit, t])

        def send_kv(layer, kind, t):
            def act(group, turn, plan):
                for edge, (j, _, _) in enumerate(plan.edges[me]):
                    if j == me:
                        kv_copy(layer, group, turn, plan, edge, kind, t).start()

            each(t, act)

        def send_q(layer, t):
            def act(group, turn, plan):
                for visit in range(len(plan.visits[me])):
                    q_copy(layer, group, turn, plan, visit, t).start()

            each(t, act)

        def forward(layer, t, depth):
            def act(group, turn, plan):
                done = set()
                for edge, (j, _, deep) in enumerate(plan.edges[me]):
                    if j != me and deep == depth:
                        for kind in range(2):
                            if j not in done:
                                kv_arrival(layer, group, plan.slots[me].index(j), kind, t).wait_recv()
                            kv_copy(layer, group, turn, plan, edge, kind, t).start()
                        done.add(j)

            each(t, act)

        def block(layer, group, plan, j, t):
            if j == me:
                at_head = lanes(group, t)
                return own[layer, 1, :, at_head], own[layer, 2, :, at_head], False
            slot = plan.slots[me].index(j)
            return kv[layer, group, slot, 0, t], kv[layer, group, slot, 1, t], False

        def serve(layer, t):
            def act(group, turn, plan):
                for slot, j in enumerate(plan.slots[me]):
                    if not any(e[0] == j for e in plan.edges[me]):
                        for kind in range(2):
                            kv_arrival(layer, group, slot, kind, t).wait_recv()
                for slot, i in enumerate(plan.guests[me]):
                    q_arrival(layer, group, slot, t).wait_recv()
                    blocks = [block(layer, group, plan, j, t) for j in plan.away[i, me]]
                    mixed, level = partial(guest[layer, group, slot, t], blocks, None)
                    note[layer, group, slot, t, pl.ds(0, HD), :] = mixed.astype(jnp.bfloat16)
                    first = level.astype(jnp.bfloat16).astype(jnp.float32)
                    rest = level - first
                    second = rest.astype(jnp.bfloat16).astype(jnp.float32)
                    third = rest - second
                    line = lax.broadcasted_iota(jnp.int32, (NOTE, ROWS), 0)
                    tail = jnp.where(
                        line == 0, first, jnp.where(line == 1, second, jnp.where(line == 2, third, 0.0))
                    )
                    note[layer, group, slot, t, pl.ds(HD, NOTE), :] = tail.astype(jnp.bfloat16)
                    o_copy(layer, group, turn, plan, slot, t).start()

            each(t, act)

        def merge(layer, t):
            place = jnp.where(layer == 1, parity_order(key_row), key_row)
            against = jnp.where(layer == 1, parity_order(query_col), query_col)
            allowed = place <= against

            def act(group, turn, plan):
                at_head = lanes(group, t)
                blocks = [block(layer, group, plan, j, t) for j in plan.home[me]]
                blocks.append((own[layer, 1, :, at_head], own[layer, 2, :, at_head], True))
                mixed, level = partial(own[layer, 0, :, at_head], blocks, allowed)
                parts = [(mixed, level)]
                for visit in range(len(plan.visits[me])):
                    o_arrival(layer, group, visit, t).wait_recv()
                    other = reply[layer, group, visit, t, pl.ds(0, HD), :].astype(jnp.float32)
                    tail = reply[layer, group, visit, t, pl.ds(HD, NOTE), :].astype(jnp.float32)
                    parts.append((other, tail[0:1] + tail[1:2] + tail[2:3]))
                if len(parts) > 1:
                    top = functools.reduce(jnp.maximum, [level for _, level in parts])
                    shares = [jnp.exp2(level - top) for _, level in parts]
                    weighed = [part * share for (part, _), share in zip(parts, shares)]
                    mixed = functools.reduce(jnp.add, weighed) / functools.reduce(jnp.add, shares)
                out[layer, :, at_head] = mixed.T.astype(jnp.bfloat16)

            each(t, act)

        def put_up(t):
            return pltpu.make_async_copy(
                out.at[0, :, round_lanes(t)], upo_ref.at[:, round_lanes(t)], put_sem.at[0]
            )

        def put_down(t):
            return pltpu.make_async_copy(
                out.at[1, my_rows, round_lanes(t)], dno_ref.at[core, :, round_lanes(t)], put_sem.at[1]
            )

        def carry_on(t):
            return remote(
                out.at[0, :, round_lanes(t)],
                carr.at[:, round_lanes(t)],
                ca_ssem.at[t],
                ca_rsem.at[t],
                {"section": lax.rem(s + 1, sections)},
            )

        other_rows = pl.ds(pl.multiple_of((1 - core) * half, half), half)

        def give_back(t):
            return remote(
                out.at[1, other_rows, round_lanes(t)],
                dno_ref.at[core, :, round_lanes(t)],
                back_ssem.at[t],
                back_rsem.at[t],
                {"replica": twin},
            )

        def given_back(t):
            return remote(
                out.at[1, other_rows, round_lanes(t)],
                dno_ref.at[1 - core, :, round_lanes(t)],
                back_ssem.at[t],
                back_rsem.at[t],
                {"replica": twin},
            )

        def mix(t):
            here = round_lanes(t)

            @pl.when(s > 0)
            def _():
                carry_on(t).wait_recv()
                reorder = jnp.where(query_col == parity_order(key_row), 1.0, 0.0).astype(jnp.bfloat16)
                moved = jnp.dot(reorder, carr[:, here], preferred_element_type=jnp.float32)
                own[1, 2, :, here] = (own[1, 2, :, here].astype(jnp.float32) + moved).astype(jnp.bfloat16)

        def early(t, c):
            for kind in range(2):
                send_kv(0, kind, t)
            send_q(0, t)
            return c

        lax.fori_loop(0, AHEAD, early, 0)
        for part in range(3):
            keep(part).wait()
            swap(part).wait_recv()

        total = 2 * rounds

        def body(step, c):
            g = step - (DEPTH - 1)

            def ranged(index, low, high, act):
                @pl.when(jnp.logical_and(index >= low, index < high))
                def _():
                    act(index)

            def mix_and_send(index):
                mix(index)
                send_kv(1, 1, index)

            ahead = g + DEPTH - 1 + AHEAD
            ranged(ahead, AHEAD, rounds, lambda i: early(i, 0))

            def keys_and_queries(index):
                send_kv(1, 0, index)
                send_q(1, index)

            ranged(ahead - rounds, 0, rounds, keys_and_queries)
            ranged(g - MIX_LAG, 0, rounds, mix_and_send)
            for depth in range(2, DEPTH + 1):
                ranged(
                    g + DEPTH + 1 - depth,
                    0,
                    total,
                    lambda i, depth=depth: forward(i // rounds, lax.rem(i, rounds), depth),
                )

            def finish(index):
                layer = index // rounds
                t = lax.rem(index, rounds)
                merge(layer, t)

                @pl.when(layer == 0)
                def _():
                    put_up(t).start()

                    @pl.when(s < sections - 1)
                    def _():
                        carry_on(t).start()

                    put_up(t).wait()

                @pl.when(layer == 1)
                def _():
                    give_back(t).start()
                    put_down(t).start()
                    put_down(t).wait()

            ranged(g - MERGE_LAG, 0, total, finish)
            ranged(g, 0, total, lambda i: serve(i // rounds, lax.rem(i, rounds)))
            return c

        lax.fori_loop(0, total + DEPTH - 1 + MERGE_LAG, body, 0)

        def sent(place, ssem, rsem, n):
            remote(place, place, ssem, rsem, {"tensor": n}).wait_send()

        for layer in range(2):
            for group, plans in enumerate(PLANS):
                turns = pl.ds(0, rounds // len(plans))
                for turn, plan in enumerate(plans):
                    for edge, (_, n, _) in enumerate(plan.edges[me]):
                        for kind in range(2):
                            sent(
                                kv.at[layer, group, 0, kind, turns],
                                kv_ssem.at[layer, group, turn, edge, kind],
                                kv_rsem.at[layer, group, 0, kind, 0],
                                n,
                            )
                    for visit, n in enumerate(plan.visits[me]):
                        sent(
                            guest.at[layer, group, 0, turns],
                            q_ssem.at[layer, group, turn, visit],
                            q_rsem.at[layer, group, 0, 0],
                            n,
                        )
                    for slot, n in enumerate(plan.guests[me]):
                        sent(
                            note.at[layer, group, slot, turns],
                            o_ssem.at[layer, group, turn, slot],
                            o_rsem.at[layer, group, 0, 0],
                            n,
                        )

        def settle(t, c):
            give_back(t).wait_send()
            given_back(t).wait_recv()

            @pl.when(s < sections - 1)
            def _():
                carry_on(t).wait_send()

            return c

        lax.fori_loop(0, rounds, settle, 0)
        for part in range(3):
            swap(part).wait_send()

    for me in range(RING):
        pl.when(z == me)(functools.partial(program, me))


def per_device(sections, up_qkv, down_qk, down_values):
    rows = up_qkv.shape[2]
    width = up_qkv.shape[3] // 3
    half = rows // 2
    groups = len(GROUPS)
    rounds = width // HD // groups
    up = up_qkv.reshape(rows, 3 * width)
    dqk = jnp.swapaxes(down_qk.reshape(half, 2, 2 * width), 0, 1)
    dv = jnp.swapaxes(down_values.reshape(half, 2, width), 0, 1)
    hbm = pl.BlockSpec(memory_space=pl.ANY)
    dma = pltpu.SemaphoreType.DMA

    def vmem(*shape):
        return pltpu.VMEM(shape, jnp.bfloat16)

    up_out, down = pl.pallas_call(
        functools.partial(relay_kernel, sections, rounds),
        name="relay",
        out_shape=(
            jax.ShapeDtypeStruct((rows, width), jnp.bfloat16),
            jax.ShapeDtypeStruct((2, half, width), jnp.bfloat16),
        ),
        in_specs=[hbm, hbm, hbm],
        out_specs=(hbm, hbm),
        scratch_shapes=[
            vmem(2, 3, rows, width),
            vmem(2, groups, SLOTS, 2, rounds, rows, HD),
            vmem(2, groups, GUESTS, rounds, rows, HD),
            vmem(2, groups, GUESTS, rounds, HD + NOTE, rows),
            vmem(2, groups, VISITS, rounds, HD + NOTE, rows),
            vmem(2, rows, width),
            vmem(rows, width),
            dma((2, groups, 2, EDGES, 2)),
            dma((2, groups, SLOTS, 2, rounds)),
            dma((2, groups, 2, VISITS)),
            dma((2, groups, GUESTS, rounds)),
            dma((2, groups, 2, GUESTS)),
            dma((2, groups, VISITS, rounds)),
            dma((rounds,)),
            dma((rounds,)),
            dma((3,)),
            dma((3,)),
            dma((rounds,)),
            dma((rounds,)),
            dma((6,)),
            dma((3,)),
        ],
        compiler_params=pltpu.CompilerParams(
            collective_id=0, has_side_effects=True, vmem_limit_bytes=46 * 1024 * 1024
        ),
    )(up, dqk, dv)
    down_out = jnp.swapaxes(down, 0, 1)
    return (
        up_out.reshape(1, 1, rows, width),
        down_out.reshape(1, 1, half, 2, width),
    )


def solution(mesh):
    placed = (
        P("section", "replica", "tensor", None),
        P("section", "replica", "tensor", None, None),
        P("section", "replica", "tensor", None, None),
    )
    return jax.shard_map(
        functools.partial(per_device, mesh.shape["section"]),
        mesh=mesh,
        in_specs=placed,
        out_specs=(placed[0], placed[1]),
        check_vma=False,
    )
```

```python
import functools
import math

import jax
import jax.numpy as jnp
from jax import lax
from jax.experimental import pallas as pl
from jax.experimental.pallas import tpu as pltpu
from jax.sharding import PartitionSpec as P

HD = 128
ROWS = 128
NOTE = 16
RING = 8
LOG2E = 1.4426950408889634
MESH = pl.DeviceIdType.MESH

GROUPS = (
    (
        ({0: (3, 1), 1: (4, 0), 2: (0, 2), 3: (0, 1), 5: (1, 0), 6: (0, 1)}, {2: (1,), 3: (5,), 4: (5,), 5: (4,), 6: (4,), 7: (4,)}),
    ),
    (
        ({0: (3, 1), 1: (4, 0), 2: (0, 2), 3: (0, 1), 5: (1, 0), 6: (0, 1)}, {2: (1,), 3: (5,), 4: (5,), 5: (4,), 6: (4,), 7: (4,)}),
        ({0: (0, 2), 1: (1, 1), 2: (2, 0), 3: (3, 0), 4: (0, 2), 5: (0, 1)}, {3: (2,), 4: (2,), 5: (0,), 6: (0,), 7: (6, 0)}),
    ),
    (
        ({0: (0, 3), 1: (0, 2), 2: (0, 1), 3: (1, 0), 4: (2, 0), 5: (0, 2), 6: (0, 1)}, {4: (3,), 5: (3,), 6: (3,), 7: (2,)}),
        ({0: (0, 2), 1: (0, 1), 2: (1, 0), 3: (2, 0), 4: (0, 2), 5: (0, 1)}, {3: (2,), 4: (2,), 5: (2,), 6: (1,), 7: (6, 1)}),
    ),
    (
        ({0: (0, 2), 1: (0, 1), 2: (1, 0), 3: (2, 0), 4: (3, 0), 5: (0, 1)}, {3: (2,), 4: (2,), 5: (2,), 6: (1,), 7: (6, 1)}),
        ({0: (0, 1), 1: (1, 0), 2: (2, 0), 3: (3, 0), 4: (0, 1), 6: (1, 0)}, {2: (1,), 3: (1,), 4: (1,), 5: (0,), 6: (5, 0), 7: (5, 0)}),
    ),
)


class Plan:
    def __init__(self, reach, visits, share, load):
        arcs = {}
        for j in range(RING):
            down, up = reach.get(j, (0, 0))
            arcs[j] = {(j + h) % RING for h in range(1, up + 1)} | {(j - h) % RING for h in range(1, down + 1)}
        needed = {j: set() for j in range(RING)}
        met = {i: {} for i in range(RING)}
        loose = []
        for i in range(RING):
            load[i] += share
            for j in range(i):
                spots = [n for n in (i, *visits.get(i, ())) if n in arcs[j] or n == j]
                assert spots, (i, j)
                loose.append((len(spots), i, j, spots))
        for _, i, j, spots in sorted(loose):
            best = min(spots, key=lambda n: load[n] + (0 if n == j or n in needed[j] else 8))
            met[i].setdefault(best, []).append(j)
            load[best] += share
            if best != j:
                needed[j].add(best)
        self.home = {i: sorted(met[i].get(i, [])) for i in range(RING)}
        self.visits = {i: [n for n in visits.get(i, ()) if n in met[i]] for i in range(RING)}
        self.away = {(i, n): sorted(met[i][n]) for i in range(RING) for n in self.visits[i]}
        self.slots = {n: [j for j in range(RING) if n in needed[j]] for n in range(RING)}
        self.guests = {n: [i for i in range(RING) if n in self.visits[i]] for n in range(RING)}
        self.edges = {n: [] for n in range(RING)}
        for j in range(RING):
            down, up = reach.get(j, (0, 0))
            for way, far in ((1, up), (-1, down)):
                last, depth = j, 0
                for h in range(1, far + 1):
                    n = (j + way * h) % RING
                    if n in needed[j]:
                        depth += 1
                        self.edges[last].append((j, n, depth))
                        last = n


def make_plans():
    load = [0] * RING
    return [[Plan(*table, 2 // len(tables), load) for table in tables] for tables in GROUPS], load


PLANS, LOAD = make_plans()
ALL = [plan for plans in PLANS for plan in plans]
SLOTS = max(len(p.slots[n]) for p in ALL for n in range(RING))
GUESTS = max(len(p.guests[n]) for p in ALL for n in range(RING))
EDGES = max(len(p.edges[n]) for p in ALL for n in range(RING))
VISITS = max(len(p.visits[n]) for p in ALL for n in range(RING))
DEPTH = max(e[2] for p in ALL for n in range(RING) for e in p.edges[n])
MERGE_LAG = 2
MIX_LAG = 4
AHEAD = 1


def relay_kernel(
    sections,
    rounds,
    up_ref,
    dqk_ref,
    dv_ref,
    upo_ref,
    dno_ref,
    own,
    kv,
    guest,
    note,
    reply,
    out,
    carr,
    raw,
    split,
    kv_ssem,
    kv_rsem,
    q_ssem,
    q_rsem,
    o_ssem,
    o_rsem,
    ca_ssem,
    ca_rsem,
    swap_ssem,
    swap_rsem,
    back_ssem,
    back_rsem,
    own_sem,
    put_sem,
):
    half = ROWS // 2
    groups = len(GROUPS)
    width = groups * rounds * HD
    wide = groups * HD
    scale = LOG2E / math.sqrt(HD)
    s = lax.axis_index("section")
    r = lax.axis_index("replica")
    z = lax.axis_index("tensor")
    core = lax.rem(r, 2)
    twin = r + 1 - 2 * core

    def remote(src, dst, ssem, rsem, device):
        return pltpu.make_async_remote_copy(
            src_ref=src, dst_ref=dst, send_sem=ssem, recv_sem=rsem, device_id=device, device_id_type=MESH
        )

    def stage(part):
        return pltpu.make_async_copy(up_ref.at[:, pl.ds(part * width, width)], own.at[0, part], own_sem.at[part])

    def fetch(part):
        source = dv_ref if part == 2 else dqk_ref.at[:, :, pl.ds(part * width, width)]
        return pltpu.make_async_copy(source, raw, own_sem.at[3])

    for part in (1, 2, 0):
        stage(part).start()
    fetch(1).start()

    barrier = pltpu.get_barrier_semaphore()
    for d in range(1, RING):
        pl.semaphore_signal(barrier, inc=1, device_id={"tensor": lax.rem(z + d, RING)}, device_id_type=MESH)
    pl.semaphore_signal(barrier, inc=1, device_id={"replica": twin}, device_id_type=MESH)
    for step in (1, sections - 1):
        pl.semaphore_signal(
            barrier, inc=1, device_id={"section": lax.rem(s + step, sections)}, device_id_type=MESH
        )
    pl.semaphore_wait(barrier, RING - 1 + 1 + 2)

    my_rows = pl.ds(pl.multiple_of(core * half, half), half)

    def swap(part):
        return remote(
            split.at[part],
            own.at[1, part, my_rows, :],
            swap_ssem.at[part],
            swap_rsem.at[part],
            {"replica": twin},
        )

    for part in range(3):
        stage(part).wait()

    def lanes(group, t):
        return pl.ds(pl.multiple_of((t * groups + group) * HD, HD), HD)

    def round_lanes(t):
        return pl.ds(pl.multiple_of(t * wide, wide), wide)

    def parity_order(index):
        return 2 * lax.rem(index, half) + index // half

    key_row = lax.broadcasted_iota(jnp.int32, (ROWS, ROWS), 0)
    query_col = lax.broadcasted_iota(jnp.int32, (ROWS, ROWS), 1)

    def unzip(part, following):
        fetch(part).wait()
        seq = jnp.where(key_row < half, core, 1 - core)
        apart = jnp.where(query_col == 2 * lax.rem(key_row, half) + seq, 1.0, 0.0).astype(jnp.bfloat16)

        def piece(t, c):
            here = round_lanes(t)
            both = raw[:, :, here].reshape(ROWS, wide)
            moved = jnp.dot(apart, both, preferred_element_type=jnp.float32).astype(jnp.bfloat16)
            own[1, part, my_rows, here] = moved[:half]
            split[part, :, here] = moved[half:]
            return c

        lax.fori_loop(0, rounds, piece, 0)
        if following is not None:
            fetch(following).start()
        swap(part).start()

    def swapped():
        for part in range(3):
            swap(part).wait_recv()

    def partial(queries, blocks, allowed):
        scores = []
        for keys, _, diagonal in blocks:
            score = lax.dot_general(
                keys, queries, (((1,), (1,)), ((), ())), preferred_element_type=jnp.float32
            )
            scores.append(jnp.where(allowed, score, -1e30) if diagonal else score)
        peak = functools.reduce(jnp.maximum, scores)
        peak = jnp.max(peak, axis=0, keepdims=True)
        weights = [jnp.exp2((score - peak) * scale) for score in scores]
        total = jnp.sum(functools.reduce(jnp.add, weights), axis=0, keepdims=True)
        mixed = None
        for weight, (_, values, _) in zip(weights, blocks):
            term = lax.dot_general(
                values,
                weight.astype(jnp.bfloat16),
                (((0,), (0,)), ((), ())),
                preferred_element_type=jnp.float32,
            )
            mixed = term if mixed is None else mixed + term
        return mixed / total, peak * scale + jnp.log2(total)

    def program(me):
        def each(t, act):
            for group, plans in enumerate(PLANS):
                for turn, plan in enumerate(plans):
                    todo = functools.partial(act, group, turn, plan)
                    if len(plans) == 1:
                        todo()
                    else:
                        pl.when(lax.rem(t, 2) == turn)(todo)

        def kv_copy(layer, group, turn, plan, edge, kind, t):
            j, n, _ = plan.edges[me][edge]
            slot = plan.slots[n].index(j)
            if j == me:
                source = own.at[layer, 1 + kind, :, lanes(group, t)]
            else:
                source = kv.at[layer, group, plan.slots[me].index(j), kind, t]
            return remote(
                source,
                kv.at[layer, group, slot, kind, t],
                kv_ssem.at[layer, group, turn, edge, kind],
                kv_rsem.at[layer, group, slot, kind, t],
                {"tensor": n},
            )

        def arrival(place, sem):
            return remote(place, place, put_sem.at[2], sem, {"tensor": (me + 1) % RING})

        def kv_arrival(layer, group, slot, kind, t):
            return arrival(kv.at[layer, group, slot, kind, t], kv_rsem.at[layer, group, slot, kind, t])

        def q_copy(layer, group, turn, plan, visit, t):
            n = plan.visits[me][visit]
            slot = plan.guests[n].index(me)
            return remote(
                own.at[layer, 0, :, lanes(group, t)],
                guest.at[layer, group, slot, t],
                q_ssem.at[layer, group, turn, visit],
                q_rsem.at[layer, group, slot, t],
                {"tensor": n},
            )

        def q_arrival(layer, group, slot, t):
            return arrival(guest.at[layer, group, slot, t], q_rsem.at[layer, group, slot, t])

        def o_copy(layer, group, turn, plan, slot, t):
            i = plan.guests[me][slot]
            visit = plan.visits[i].index(me)
            return remote(
                note.at[layer, group, slot, t],
                reply.at[layer, group, visit, t],
                o_ssem.at[layer, group, turn, slot],
                o_rsem.at[layer, group, visit, t],
                {"tensor": i},
            )

        def o_arrival(layer, group, visit, t):
            return arrival(reply.at[layer, group, visit, t], o_rsem.at[layer, group, visit, t])

        def send_kv(layer, kind, t):
            def act(group, turn, plan):
                for edge, (j, _, _) in enumerate(plan.edges[me]):
                    if j == me:
                        kv_copy(layer, group, turn, plan, edge, kind, t).start()

            each(t, act)

        def send_q(layer, t):
            def act(group, turn, plan):
                for visit in range(len(plan.visits[me])):
                    q_copy(layer, group, turn, plan, visit, t).start()

            each(t, act)

        def forward(layer, t, depth):
            def act(group, turn, plan):
                done = set()
                for edge, (j, _, deep) in enumerate(plan.edges[me]):
                    if j != me and deep == depth:
                        for kind in range(2):
                            if j not in done:
                                kv_arrival(layer, group, plan.slots[me].index(j), kind, t).wait_recv()
                            kv_copy(layer, group, turn, plan, edge, kind, t).start()
                        done.add(j)

            each(t, act)

        def block(layer, group, plan, j, t):
            if j == me:
                at_head = lanes(group, t)
                return own[layer, 1, :, at_head], own[layer, 2, :, at_head], False
            slot = plan.slots[me].index(j)
            return kv[layer, group, slot, 0, t], kv[layer, group, slot, 1, t], False

        def serve(layer, t):
            def act(group, turn, plan):
                for slot, j in enumerate(plan.slots[me]):
                    if not any(e[0] == j for e in plan.edges[me]):
                        for kind in range(2):
                            kv_arrival(layer, group, slot, kind, t).wait_recv()
                for slot, i in enumerate(plan.guests[me]):
                    q_arrival(layer, group, slot, t).wait_recv()
                    blocks = [block(layer, group, plan, j, t) for j in plan.away[i, me]]
                    mixed, level = partial(guest[layer, group, slot, t], blocks, None)
                    note[layer, group, slot, t, pl.ds(0, HD), :] = mixed.astype(jnp.bfloat16)
                    first = level.astype(jnp.bfloat16).astype(jnp.float32)
                    rest = level - first
                    second = rest.astype(jnp.bfloat16).astype(jnp.float32)
                    third = rest - second
                    line = lax.broadcasted_iota(jnp.int32, (NOTE, ROWS), 0)
                    tail = jnp.where(
                        line == 0, first, jnp.where(line == 1, second, jnp.where(line == 2, third, 0.0))
                    )
                    note[layer, group, slot, t, pl.ds(HD, NOTE), :] = tail.astype(jnp.bfloat16)
                    o_copy(layer, group, turn, plan, slot, t).start()

            each(t, act)

        def merge(layer, t):
            place = jnp.where(layer == 1, parity_order(key_row), key_row)
            against = jnp.where(layer == 1, parity_order(query_col), query_col)
            allowed = place <= against

            def act(group, turn, plan):
                at_head = lanes(group, t)
                blocks = [block(layer, group, plan, j, t) for j in plan.home[me]]
                blocks.append((own[layer, 1, :, at_head], own[layer, 2, :, at_head], True))
                mixed, level = partial(own[layer, 0, :, at_head], blocks, allowed)
                parts = [(mixed, level)]
                for visit in range(len(plan.visits[me])):
                    o_arrival(layer, group, visit, t).wait_recv()
                    other = reply[layer, group, visit, t, pl.ds(0, HD), :].astype(jnp.float32)
                    tail = reply[layer, group, visit, t, pl.ds(HD, NOTE), :].astype(jnp.float32)
                    parts.append((other, tail[0:1] + tail[1:2] + tail[2:3]))
                if len(parts) > 1:
                    top = functools.reduce(jnp.maximum, [level for _, level in parts])
                    shares = [jnp.exp2(level - top) for _, level in parts]
                    weighed = [part * share for (part, _), share in zip(parts, shares)]
                    mixed = functools.reduce(jnp.add, weighed) / functools.reduce(jnp.add, shares)
                out[layer, :, at_head] = mixed.T.astype(jnp.bfloat16)

            each(t, act)

        def put_up(t):
            return pltpu.make_async_copy(
                out.at[0, :, round_lanes(t)], upo_ref.at[:, round_lanes(t)], put_sem.at[0]
            )

        def put_down(t):
            return pltpu.make_async_copy(
                out.at[1, my_rows, round_lanes(t)], dno_ref.at[core, :, round_lanes(t)], put_sem.at[1]
            )

        def carry_on(t):
            return remote(
                out.at[0, :, round_lanes(t)],
                carr.at[:, round_lanes(t)],
                ca_ssem.at[t],
                ca_rsem.at[t],
                {"section": lax.rem(s + 1, sections)},
            )

        other_rows = pl.ds(pl.multiple_of((1 - core) * half, half), half)

        def give_back(t):
            return remote(
                out.at[1, other_rows, round_lanes(t)],
                dno_ref.at[core, :, round_lanes(t)],
                back_ssem.at[t],
                back_rsem.at[t],
                {"replica": twin},
            )

        def given_back(t):
            return remote(
                out.at[1, other_rows, round_lanes(t)],
                dno_ref.at[1 - core, :, round_lanes(t)],
                back_ssem.at[t],
                back_rsem.at[t],
                {"replica": twin},
            )

        def mix(t):
            here = round_lanes(t)

            @pl.when(s > 0)
            def _():
                carry_on(t).wait_recv()
                reorder = jnp.where(query_col == parity_order(key_row), 1.0, 0.0).astype(jnp.bfloat16)
                moved = jnp.dot(reorder, carr[:, here], preferred_element_type=jnp.float32)
                own[1, 2, :, here] = (own[1, 2, :, here].astype(jnp.float32) + moved).astype(jnp.bfloat16)

        def early(t, c):
            for kind in range(2):
                send_kv(0, kind, t)
            send_q(0, t)
            return c

        lax.fori_loop(0, AHEAD, early, 0)

        total = 2 * rounds

        def body(step, c):
            g = step - (DEPTH - 1)
            order = (1, 0, 2, None)
            for turn in range(3):
                pl.when(step == turn)(functools.partial(unzip, order[turn], order[turn + 1]))
            pl.when(step == 5)(swapped)

            def ranged(index, low, high, act):
                @pl.when(jnp.logical_and(index >= low, index < high))
                def _():
                    act(index)

            def mix_and_send(index):
                mix(index)
                send_kv(1, 1, index)

            ahead = g + DEPTH - 1 + AHEAD
            ranged(ahead, AHEAD, rounds, lambda i: early(i, 0))

            def keys_and_queries(index):
                send_kv(1, 0, index)
                send_q(1, index)

            ranged(ahead - rounds, 0, rounds, keys_and_queries)
            ranged(g - MIX_LAG, 0, rounds, mix_and_send)
            for depth in range(2, DEPTH + 1):
                ranged(
                    g + DEPTH + 1 - depth,
                    0,
                    total,
                    lambda i, depth=depth: forward(i // rounds, lax.rem(i, rounds), depth),
                )

            def finish(index):
                layer = index // rounds
                t = lax.rem(index, rounds)
                merge(layer, t)

                @pl.when(layer == 0)
                def _():
                    put_up(t).start()

                    @pl.when(s < sections - 1)
                    def _():
                        carry_on(t).start()

                    put_up(t).wait()

                @pl.when(layer == 1)
                def _():
                    give_back(t).start()
                    put_down(t).start()
                    put_down(t).wait()

            ranged(g - MERGE_LAG, 0, total, finish)
            ranged(g, 0, total, lambda i: serve(i // rounds, lax.rem(i, rounds)))
            return c

        lax.fori_loop(0, total + DEPTH - 1 + MERGE_LAG, body, 0)

        def sent(place, ssem, rsem, n):
            remote(place, place, ssem, rsem, {"tensor": n}).wait_send()

        for layer in range(2):
            for group, plans in enumerate(PLANS):
                turns = pl.ds(0, rounds // len(plans))
                for turn, plan in enumerate(plans):
                    for edge, (_, n, _) in enumerate(plan.edges[me]):
                        for kind in range(2):
                            sent(
                                kv.at[layer, group, 0, kind, turns],
                                kv_ssem.at[layer, group, turn, edge, kind],
                                kv_rsem.at[layer, group, 0, kind, 0],
                                n,
                            )
                    for visit, n in enumerate(plan.visits[me]):
                        sent(
                            guest.at[layer, group, 0, turns],
                            q_ssem.at[layer, group, turn, visit],
                            q_rsem.at[layer, group, 0, 0],
                            n,
                        )
                    for slot, n in enumerate(plan.guests[me]):
                        sent(
                            note.at[layer, group, slot, turns],
                            o_ssem.at[layer, group, turn, slot],
                            o_rsem.at[layer, group, 0, 0],
                            n,
                        )

        def settle(t, c):
            give_back(t).wait_send()
            given_back(t).wait_recv()

            @pl.when(s < sections - 1)
            def _():
                carry_on(t).wait_send()

            return c

        lax.fori_loop(0, rounds, settle, 0)
        for part in range(3):
            swap(part).wait_send()

    for me in range(RING):
        pl.when(z == me)(functools.partial(program, me))


def per_device(sections, up_qkv, down_qk, down_values):
    rows = up_qkv.shape[2]
    width = up_qkv.shape[3] // 3
    half = rows // 2
    groups = len(GROUPS)
    rounds = width // HD // groups
    up = up_qkv.reshape(rows, 3 * width)
    dqk = down_qk.reshape(half, 2, 2 * width)
    dv = down_values.reshape(half, 2, width)
    hbm = pl.BlockSpec(memory_space=pl.ANY)
    dma = pltpu.SemaphoreType.DMA

    def vmem(*shape):
        return pltpu.VMEM(shape, jnp.bfloat16)

    up_out, down = pl.pallas_call(
        functools.partial(relay_kernel, sections, rounds),
        name="relay",
        out_shape=(
            jax.ShapeDtypeStruct((rows, width), jnp.bfloat16),
            jax.ShapeDtypeStruct((2, half, width), jnp.bfloat16),
        ),
        in_specs=[hbm, hbm, hbm],
        out_specs=(hbm, hbm),
        scratch_shapes=[
            vmem(2, 3, rows, width),
            vmem(2, groups, SLOTS, 2, rounds, rows, HD),
            vmem(2, groups, GUESTS, rounds, rows, HD),
            vmem(2, groups, GUESTS, rounds, HD + NOTE, rows),
            vmem(2, groups, VISITS, rounds, HD + NOTE, rows),
            vmem(2, rows, width),
            vmem(rows, width),
            vmem(half, 2, width),
            vmem(3, half, width),
            dma((2, groups, 2, EDGES, 2)),
            dma((2, groups, SLOTS, 2, rounds)),
            dma((2, groups, 2, VISITS)),
            dma((2, groups, GUESTS, rounds)),
            dma((2, groups, 2, GUESTS)),
            dma((2, groups, VISITS, rounds)),
            dma((rounds,)),
            dma((rounds,)),
            dma((3,)),
            dma((3,)),
            dma((rounds,)),
            dma((rounds,)),
            dma((4,)),
            dma((3,)),
        ],
        compiler_params=pltpu.CompilerParams(
            collective_id=0, has_side_effects=True, vmem_limit_bytes=49 * 1024 * 1024
        ),
    )(up, dqk, dv)
    down_out = jnp.swapaxes(down, 0, 1)
    return (
        up_out.reshape(1, 1, rows, width),
        down_out.reshape(1, 1, half, 2, width),
    )


def solution(mesh):
    placed = (
        P("section", "replica", "tensor", None),
        P("section", "replica", "tensor", None, None),
        P("section", "replica", "tensor", None, None),
    )
    return jax.shard_map(
        functools.partial(per_device, mesh.shape["section"]),
        mesh=mesh,
        in_specs=placed,
        out_specs=(placed[0], placed[1]),
        check_vma=False,
    )
```

```python
import functools
import math

import jax
import jax.numpy as jnp
from jax import lax
from jax.experimental import pallas as pl
from jax.experimental.pallas import tpu as pltpu
from jax.sharding import PartitionSpec as P

HD = 128
ROWS = 128
NOTE = 16
RING = 8
LOG2E = 1.4426950408889634
MESH = pl.DeviceIdType.MESH

GROUPS = (
    (
        ({0: (3, 1), 1: (4, 0), 2: (0, 2), 3: (0, 1), 5: (1, 0), 6: (0, 1)}, {2: (1,), 3: (5,), 4: (5,), 5: (4,), 6: (4,), 7: (4,)}),
    ),
    (
        ({0: (3, 1), 1: (4, 0), 2: (0, 2), 3: (0, 1), 5: (1, 0), 6: (0, 1)}, {2: (1,), 3: (5,), 4: (5,), 5: (4,), 6: (4,), 7: (4,)}),
        ({0: (0, 2), 1: (1, 1), 2: (2, 0), 3: (3, 0), 4: (0, 2), 5: (0, 1)}, {3: (2,), 4: (2,), 5: (0,), 6: (0,), 7: (6, 0)}),
    ),
    (
        ({0: (0, 3), 1: (0, 2), 2: (0, 1), 3: (1, 0), 4: (2, 0), 5: (0, 2), 6: (0, 1)}, {4: (3,), 5: (3,), 6: (3,), 7: (2,)}),
        ({0: (0, 2), 1: (0, 1), 2: (1, 0), 3: (2, 0), 4: (0, 2), 5: (0, 1)}, {3: (2,), 4: (2,), 5: (2,), 6: (1,), 7: (6, 1)}),
    ),
    (
        ({0: (0, 2), 1: (0, 1), 2: (1, 0), 3: (2, 0), 4: (3, 0), 5: (0, 1)}, {3: (2,), 4: (2,), 5: (2,), 6: (1,), 7: (6, 1)}),
        ({0: (0, 1), 1: (1, 0), 2: (2, 0), 3: (3, 0), 4: (0, 1), 6: (1, 0)}, {2: (1,), 3: (1,), 4: (1,), 5: (0,), 6: (5, 0), 7: (5, 0)}),
    ),
)


class Plan:
    def __init__(self, reach, visits, share, load):
        arcs = {}
        for j in range(RING):
            down, up = reach.get(j, (0, 0))
            arcs[j] = {(j + h) % RING for h in range(1, up + 1)} | {(j - h) % RING for h in range(1, down + 1)}
        needed = {j: set() for j in range(RING)}
        met = {i: {} for i in range(RING)}
        loose = []
        for i in range(RING):
            load[i] += share
            for j in range(i):
                spots = [n for n in (i, *visits.get(i, ())) if n in arcs[j] or n == j]
                assert spots, (i, j)
                loose.append((len(spots), i, j, spots))
        for _, i, j, spots in sorted(loose):
            best = min(spots, key=lambda n: load[n] + (0 if n == j or n in needed[j] else 8))
            met[i].setdefault(best, []).append(j)
            load[best] += share
            if best != j:
                needed[j].add(best)
        self.home = {i: sorted(met[i].get(i, [])) for i in range(RING)}
        self.visits = {i: [n for n in visits.get(i, ()) if n in met[i]] for i in range(RING)}
        self.away = {(i, n): sorted(met[i][n]) for i in range(RING) for n in self.visits[i]}
        self.slots = {n: [j for j in range(RING) if n in needed[j]] for n in range(RING)}
        self.guests = {n: [i for i in range(RING) if n in self.visits[i]] for n in range(RING)}
        self.edges = {n: [] for n in range(RING)}
        for j in range(RING):
            down, up = reach.get(j, (0, 0))
            for way, far in ((1, up), (-1, down)):
                last, depth = j, 0
                for h in range(1, far + 1):
                    n = (j + way * h) % RING
                    if n in needed[j]:
                        depth += 1
                        self.edges[last].append((j, n, depth))
                        last = n


def make_plans():
    load = [0] * RING
    return [[Plan(*table, 2 // len(tables), load) for table in tables] for tables in GROUPS], load


PLANS, LOAD = make_plans()
ALL = [plan for plans in PLANS for plan in plans]
SLOTS = max(len(p.slots[n]) for p in ALL for n in range(RING))
GUESTS = max(len(p.guests[n]) for p in ALL for n in range(RING))
EDGES = max(len(p.edges[n]) for p in ALL for n in range(RING))
VISITS = max(len(p.visits[n]) for p in ALL for n in range(RING))
DEPTH = max(e[2] for p in ALL for n in range(RING) for e in p.edges[n])
MERGE_LAG = 2
MIX_LAG = 4
AHEAD = 1


def relay_kernel(
    sections,
    rounds,
    up_ref,
    dqk_ref,
    dv_ref,
    upo_ref,
    dno_ref,
    own,
    kv,
    guest,
    note,
    reply,
    out,
    carr,
    raw,
    split,
    kv_ssem,
    kv_rsem,
    q_ssem,
    q_rsem,
    o_ssem,
    o_rsem,
    ca_ssem,
    ca_rsem,
    swap_ssem,
    swap_rsem,
    back_ssem,
    back_rsem,
    own_sem,
    put_sem,
):
    half = ROWS // 2
    groups = len(GROUPS)
    width = groups * rounds * HD
    wide = groups * HD
    scale = LOG2E / math.sqrt(HD)
    s = lax.axis_index("section")
    r = lax.axis_index("replica")
    z = lax.axis_index("tensor")
    core = lax.rem(r, 2)
    twin = r + 1 - 2 * core

    def remote(src, dst, ssem, rsem, device):
        return pltpu.make_async_remote_copy(
            src_ref=src, dst_ref=dst, send_sem=ssem, recv_sem=rsem, device_id=device, device_id_type=MESH
        )

    def stage(part):
        return pltpu.make_async_copy(up_ref.at[:, pl.ds(part * width, width)], own.at[0, part], own_sem.at[part])

    def fetch(part):
        source = dv_ref if part == 2 else dqk_ref.at[:, :, pl.ds(part * width, width)]
        return pltpu.make_async_copy(source, raw, own_sem.at[3])

    for part in (1, 2, 0):
        stage(part).start()
    fetch(1).start()

    barrier = pltpu.get_barrier_semaphore()
    for d in range(1, RING):
        pl.semaphore_signal(barrier, inc=1, device_id={"tensor": lax.rem(z + d, RING)}, device_id_type=MESH)
    pl.semaphore_signal(barrier, inc=1, device_id={"replica": twin}, device_id_type=MESH)
    for step in (1, sections - 1):
        pl.semaphore_signal(
            barrier, inc=1, device_id={"section": lax.rem(s + step, sections)}, device_id_type=MESH
        )
    pl.semaphore_wait(barrier, RING - 1 + 1 + 2)

    my_rows = pl.ds(pl.multiple_of(core * half, half), half)

    def swap(part):
        return remote(
            split.at[part],
            own.at[1, part, my_rows, :],
            swap_ssem.at[part],
            swap_rsem.at[part],
            {"replica": twin},
        )

    for part in range(3):
        stage(part).wait()

    def lanes(group, t):
        return pl.ds(pl.multiple_of((t * groups + group) * HD, HD), HD)

    def round_lanes(t):
        return pl.ds(pl.multiple_of(t * wide, wide), wide)

    def parity_order(index):
        return 2 * lax.rem(index, half) + index // half

    key_row = lax.broadcasted_iota(jnp.int32, (ROWS, ROWS), 0)
    query_col = lax.broadcasted_iota(jnp.int32, (ROWS, ROWS), 1)

    def unzip(part, following):
        fetch(part).wait()
        seq = jnp.where(key_row < half, core, 1 - core)
        apart = jnp.where(query_col == 2 * lax.rem(key_row, half) + seq, 1.0, 0.0).astype(jnp.bfloat16)

        def piece(t, c):
            here = round_lanes(t)
            both = raw[:, :, here].reshape(ROWS, wide)
            moved = jnp.dot(apart, both, preferred_element_type=jnp.float32).astype(jnp.bfloat16)
            own[1, part, my_rows, here] = moved[:half]
            split[part, :, here] = moved[half:]
            return c

        lax.fori_loop(0, rounds, piece, 0)
        if following is not None:
            fetch(following).start()
        swap(part).start()

    def swapped():
        for part in range(3):
            swap(part).wait_recv()

    def partial(queries, blocks, allowed):
        scores = []
        for keys, _, diagonal in blocks:
            score = lax.dot_general(
                keys, queries, (((1,), (1,)), ((), ())), preferred_element_type=jnp.float32
            )
            scores.append(jnp.where(allowed, score, -1e30) if diagonal else score)
        peak = functools.reduce(jnp.maximum, scores)
        peak = jnp.max(peak, axis=0, keepdims=True)
        weights = [jnp.exp2((score - peak) * scale) for score in scores]
        total = jnp.sum(functools.reduce(jnp.add, weights), axis=0, keepdims=True)
        mixed = None
        for weight, (_, values, _) in zip(weights, blocks):
            term = lax.dot_general(
                values,
                weight.astype(jnp.bfloat16),
                (((0,), (0,)), ((), ())),
                preferred_element_type=jnp.float32,
            )
            mixed = term if mixed is None else mixed + term
        return mixed / total, peak * scale + jnp.log2(total)

    def program(me):
        def each(t, act):
            for group, plans in enumerate(PLANS):
                for turn, plan in enumerate(plans):
                    todo = functools.partial(act, group, turn, plan)
                    if len(plans) == 1:
                        todo()
                    else:
                        pl.when(lax.rem(t, 2) == turn)(todo)

        def kv_copy(layer, group, turn, plan, edge, kind, t):
            j, n, _ = plan.edges[me][edge]
            slot = plan.slots[n].index(j)
            if j == me:
                source = own.at[layer, 1 + kind, :, lanes(group, t)]
            else:
                source = kv.at[layer, group, plan.slots[me].index(j), kind, t]
            return remote(
                source,
                kv.at[layer, group, slot, kind, t],
                kv_ssem.at[layer, group, turn, edge, kind],
                kv_rsem.at[layer, group, slot, kind, t],
                {"tensor": n},
            )

        def arrival(place, sem):
            return remote(place, place, put_sem.at[2], sem, {"tensor": (me + 1) % RING})

        def kv_arrival(layer, group, slot, kind, t):
            return arrival(kv.at[layer, group, slot, kind, t], kv_rsem.at[layer, group, slot, kind, t])

        def q_copy(layer, group, turn, plan, visit, t):
            n = plan.visits[me][visit]
            slot = plan.guests[n].index(me)
            return remote(
                own.at[layer, 0, :, lanes(group, t)],
                guest.at[layer, group, slot, t],
                q_ssem.at[layer, group, turn, visit],
                q_rsem.at[layer, group, slot, t],
                {"tensor": n},
            )

        def q_arrival(layer, group, slot, t):
            return arrival(guest.at[layer, group, slot, t], q_rsem.at[layer, group, slot, t])

        def o_copy(layer, group, turn, plan, slot, t):
            i = plan.guests[me][slot]
            visit = plan.visits[i].index(me)
            return remote(
                note.at[layer, group, slot, t],
                reply.at[layer, group, visit, t],
                o_ssem.at[layer, group, turn, slot],
                o_rsem.at[layer, group, visit, t],
                {"tensor": i},
            )

        def o_arrival(layer, group, visit, t):
            return arrival(reply.at[layer, group, visit, t], o_rsem.at[layer, group, visit, t])

        def send_kv(layer, kind, t):
            def act(group, turn, plan):
                for edge, (j, _, _) in enumerate(plan.edges[me]):
                    if j == me:
                        kv_copy(layer, group, turn, plan, edge, kind, t).start()

            each(t, act)

        def send_q(layer, t):
            def act(group, turn, plan):
                for visit in range(len(plan.visits[me])):
                    q_copy(layer, group, turn, plan, visit, t).start()

            each(t, act)

        def forward(layer, t, depth):
            def act(group, turn, plan):
                done = set()
                for edge, (j, _, deep) in enumerate(plan.edges[me]):
                    if j != me and deep == depth:
                        for kind in range(2):
                            if j not in done:
                                kv_arrival(layer, group, plan.slots[me].index(j), kind, t).wait_recv()
                            kv_copy(layer, group, turn, plan, edge, kind, t).start()
                        done.add(j)

            each(t, act)

        def block(layer, group, plan, j, t):
            if j == me:
                at_head = lanes(group, t)
                return own[layer, 1, :, at_head], own[layer, 2, :, at_head], False
            slot = plan.slots[me].index(j)
            return kv[layer, group, slot, 0, t], kv[layer, group, slot, 1, t], False

        def serve(layer, t):
            def act(group, turn, plan):
                for slot, j in enumerate(plan.slots[me]):
                    if not any(e[0] == j for e in plan.edges[me]):
                        for kind in range(2):
                            kv_arrival(layer, group, slot, kind, t).wait_recv()
                for slot, i in enumerate(plan.guests[me]):
                    q_arrival(layer, group, slot, t).wait_recv()
                    blocks = [block(layer, group, plan, j, t) for j in plan.away[i, me]]
                    mixed, level = partial(guest[layer, group, slot, t], blocks, None)
                    note[layer, group, slot, t, pl.ds(0, HD), :] = mixed.astype(jnp.bfloat16)
                    first = level.astype(jnp.bfloat16).astype(jnp.float32)
                    rest = level - first
                    second = rest.astype(jnp.bfloat16).astype(jnp.float32)
                    third = rest - second
                    line = lax.broadcasted_iota(jnp.int32, (NOTE, ROWS), 0)
                    tail = jnp.where(
                        line == 0, first, jnp.where(line == 1, second, jnp.where(line == 2, third, 0.0))
                    )
                    note[layer, group, slot, t, pl.ds(HD, NOTE), :] = tail.astype(jnp.bfloat16)
                    o_copy(layer, group, turn, plan, slot, t).start()

            each(t, act)

        def merge(layer, t):
            place = jnp.where(layer == 1, parity_order(key_row), key_row)
            against = jnp.where(layer == 1, parity_order(query_col), query_col)
            allowed = place <= against

            def act(group, turn, plan):
                at_head = lanes(group, t)
                blocks = [block(layer, group, plan, j, t) for j in plan.home[me]]
                blocks.append((own[layer, 1, :, at_head], own[layer, 2, :, at_head], True))
                mixed, level = partial(own[layer, 0, :, at_head], blocks, allowed)
                parts = [(mixed, level)]
                for visit in range(len(plan.visits[me])):
                    o_arrival(layer, group, visit, t).wait_recv()
                    other = reply[layer, group, visit, t, pl.ds(0, HD), :].astype(jnp.float32)
                    tail = reply[layer, group, visit, t, pl.ds(HD, NOTE), :].astype(jnp.float32)
                    parts.append((other, tail[0:1] + tail[1:2] + tail[2:3]))
                if len(parts) > 1:
                    top = functools.reduce(jnp.maximum, [level for _, level in parts])
                    shares = [jnp.exp2(level - top) for _, level in parts]
                    weighed = [part * share for (part, _), share in zip(parts, shares)]
                    mixed = functools.reduce(jnp.add, weighed) / functools.reduce(jnp.add, shares)
                out[layer, :, at_head] = mixed.T.astype(jnp.bfloat16)

            each(t, act)

        def put_up(t):
            return pltpu.make_async_copy(
                out.at[0, :, round_lanes(t)], upo_ref.at[:, round_lanes(t)], put_sem.at[0]
            )

        def put_down(t):
            return pltpu.make_async_copy(
                out.at[1, my_rows, round_lanes(t)], dno_ref.at[core, :, round_lanes(t)], put_sem.at[1]
            )

        def carry_on(t):
            return remote(
                out.at[0, :, round_lanes(t)],
                carr.at[:, round_lanes(t)],
                ca_ssem.at[t],
                ca_rsem.at[t],
                {"section": lax.rem(s + 1, sections)},
            )

        other_rows = pl.ds(pl.multiple_of((1 - core) * half, half), half)

        def give_back(t):
            return remote(
                out.at[1, other_rows, round_lanes(t)],
                dno_ref.at[core, :, round_lanes(t)],
                back_ssem.at[t],
                back_rsem.at[t],
                {"replica": twin},
            )

        def given_back(t):
            return remote(
                out.at[1, other_rows, round_lanes(t)],
                dno_ref.at[1 - core, :, round_lanes(t)],
                back_ssem.at[t],
                back_rsem.at[t],
                {"replica": twin},
            )

        def mix(t):
            here = round_lanes(t)

            @pl.when(s > 0)
            def _():
                carry_on(t).wait_recv()
                reorder = jnp.where(query_col == parity_order(key_row), 1.0, 0.0).astype(jnp.bfloat16)
                moved = jnp.dot(reorder, carr[:, here], preferred_element_type=jnp.float32)
                own[1, 2, :, here] = (own[1, 2, :, here].astype(jnp.float32) + moved).astype(jnp.bfloat16)

        def early(t, c):
            for kind in range(2):
                send_kv(0, kind, t)
            send_q(0, t)
            return c

        lax.fori_loop(0, AHEAD, early, 0)

        total = 2 * rounds

        def body(step, c):
            g = step - (DEPTH - 1)
            pl.when(step == 6)(swapped)

            def ranged(index, low, high, act):
                @pl.when(jnp.logical_and(index >= low, index < high))
                def _():
                    act(index)

            def mix_and_send(index):
                mix(index)
                send_kv(1, 1, index)

            ahead = g + DEPTH - 1 + AHEAD
            ranged(ahead, AHEAD, rounds, lambda i: early(i, 0))

            def keys_and_queries(index):
                send_kv(1, 0, index)
                send_q(1, index)

            ranged(ahead - rounds, 0, rounds, keys_and_queries)
            ranged(g - MIX_LAG, 0, rounds, mix_and_send)
            for depth in range(2, DEPTH + 1):
                ranged(
                    g + DEPTH + 1 - depth,
                    0,
                    total,
                    lambda i, depth=depth: forward(i // rounds, lax.rem(i, rounds), depth),
                )

            order = (1, 0, 2, None)
            for turn in range(3):
                pl.when(step == turn + 2)(functools.partial(unzip, order[turn], order[turn + 1]))

            def finish(index):
                layer = index // rounds
                t = lax.rem(index, rounds)
                merge(layer, t)

                @pl.when(layer == 0)
                def _():
                    put_up(t).start()

                    @pl.when(s < sections - 1)
                    def _():
                        carry_on(t).start()

                    put_up(t).wait()

                @pl.when(layer == 1)
                def _():
                    give_back(t).start()
                    put_down(t).start()
                    put_down(t).wait()

            ranged(g - MERGE_LAG, 0, total, finish)
            ranged(g, 0, total, lambda i: serve(i // rounds, lax.rem(i, rounds)))
            return c

        lax.fori_loop(0, total + DEPTH - 1 + MERGE_LAG, body, 0)

        def sent(place, ssem, rsem, n):
            remote(place, place, ssem, rsem, {"tensor": n}).wait_send()

        for layer in range(2):
            for group, plans in enumerate(PLANS):
                turns = pl.ds(0, rounds // len(plans))
                for turn, plan in enumerate(plans):
                    for edge, (_, n, _) in enumerate(plan.edges[me]):
                        for kind in range(2):
                            sent(
                                kv.at[layer, group, 0, kind, turns],
                                kv_ssem.at[layer, group, turn, edge, kind],
                                kv_rsem.at[layer, group, 0, kind, 0],
                                n,
                            )
                    for visit, n in enumerate(plan.visits[me]):
                        sent(
                            guest.at[layer, group, 0, turns],
                            q_ssem.at[layer, group, turn, visit],
                            q_rsem.at[layer, group, 0, 0],
                            n,
                        )
                    for slot, n in enumerate(plan.guests[me]):
                        sent(
                            note.at[layer, group, slot, turns],
                            o_ssem.at[layer, group, turn, slot],
                            o_rsem.at[layer, group, 0, 0],
                            n,
                        )

        def settle(t, c):
            give_back(t).wait_send()
            given_back(t).wait_recv()

            @pl.when(s < sections - 1)
            def _():
                carry_on(t).wait_send()

            return c

        lax.fori_loop(0, rounds, settle, 0)
        for part in range(3):
            swap(part).wait_send()

    for me in range(RING):
        pl.when(z == me)(functools.partial(program, me))


def per_device(sections, up_qkv, down_qk, down_values):
    rows = up_qkv.shape[2]
    width = up_qkv.shape[3] // 3
    half = rows // 2
    groups = len(GROUPS)
    rounds = width // HD // groups
    up = up_qkv.reshape(rows, 3 * width)
    dqk = down_qk.reshape(half, 2, 2 * width)
    dv = down_values.reshape(half, 2, width)
    hbm = pl.BlockSpec(memory_space=pl.ANY)
    dma = pltpu.SemaphoreType.DMA

    def vmem(*shape):
        return pltpu.VMEM(shape, jnp.bfloat16)

    up_out, down = pl.pallas_call(
        functools.partial(relay_kernel, sections, rounds),
        name="relay",
        out_shape=(
            jax.ShapeDtypeStruct((rows, width), jnp.bfloat16),
            jax.ShapeDtypeStruct((2, half, width), jnp.bfloat16),
        ),
        in_specs=[hbm, hbm, hbm],
        out_specs=(hbm, hbm),
        scratch_shapes=[
            vmem(2, 3, rows, width),
            vmem(2, groups, SLOTS, 2, rounds, rows, HD),
            vmem(2, groups, GUESTS, rounds, rows, HD),
            vmem(2, groups, GUESTS, rounds, HD + NOTE, rows),
            vmem(2, groups, VISITS, rounds, HD + NOTE, rows),
            vmem(2, rows, width),
            vmem(rows, width),
            vmem(half, 2, width),
            vmem(3, half, width),
            dma((2, groups, 2, EDGES, 2)),
            dma((2, groups, SLOTS, 2, rounds)),
            dma((2, groups, 2, VISITS)),
            dma((2, groups, GUESTS, rounds)),
            dma((2, groups, 2, GUESTS)),
            dma((2, groups, VISITS, rounds)),
            dma((rounds,)),
            dma((rounds,)),
            dma((3,)),
            dma((3,)),
            dma((rounds,)),
            dma((rounds,)),
            dma((4,)),
            dma((3,)),
        ],
        compiler_params=pltpu.CompilerParams(
            collective_id=0, has_side_effects=True, vmem_limit_bytes=49 * 1024 * 1024
        ),
    )(up, dqk, dv)
    down_out = jnp.swapaxes(down, 0, 1)
    return (
        up_out.reshape(1, 1, rows, width),
        down_out.reshape(1, 1, half, 2, width),
    )


def solution(mesh):
    placed = (
        P("section", "replica", "tensor", None),
        P("section", "replica", "tensor", None, None),
        P("section", "replica", "tensor", None, None),
    )
    return jax.shard_map(
        functools.partial(per_device, mesh.shape["section"]),
        mesh=mesh,
        in_specs=placed,
        out_specs=(placed[0], placed[1]),
        check_vma=False,
    )
```
